128 devices in a mesh: grp: 32 (over x_hi, z, y), tp: 4 (over x_lo, core).
Axes of the slice: x: 4 (x_hi: 2, x_lo: 2; x = x_hi * 2 + x_lo), y: 4, z: 4, core: 2. Of those that a mesh axis runs over, the one named last changes fastest.
Arguments:
- hidden_in: bfloat16 [512, 5120], P('grp', 'tp'), may hold values from -70 to 70
- cache_lengths: int32 [512], P('grp'), may hold values from 160 to 1280, as said below
- in_gain: float32 [5120], replicated, may hold values from 0.1 to 1.9
- post_gain: float32 [5120], replicated, may hold values from 0.1 to 1.9
- w_query: bfloat16 [5120, 2560], P(None, 'tp'), may hold values from -0.078125 to 0.078125
- b_query: float32 [2560], P('tp'), may hold values from -5 to 5
- b_key: float32 [512], P('tp'), may hold values from -5 to 5
- b_value: float32 [512], P('tp'), may hold values from -3 to 3
- w_out: bfloat16 [2560, 5120], P('tp'), may hold values from -0.75 to 0.75
- key_cache: bfloat16 [512, 4, 1280, 128], P('grp', 'tp'), may hold values from -500 to 500
- value_cache: bfloat16 [512, 4, 1280, 128], P('grp', 'tp'), may hold values from -6 to 6
- next_key_weight: bfloat16 [5120, 512], P(('grp', 'tp')), may hold values from -0.078125 to 0.078125
- next_w_value: bfloat16 [5120, 512], P(('grp', 'tp')), may hold values from -0.078125 to 0.078125
Outputs:
- attended: bfloat16 [512, 5120], P('grp', 'tp')
- normed: bfloat16 [512, 5120], P('grp', 'tp')
- key_weight_out: bfloat16 [5120, 512], P(None, 'tp')
- value_weight_out: bfloat16 [5120, 512], P(None, 'tp')
The draws below stay inside these ranges and needn't reach their ends.
Inputs may be any that keep to these rules, and one draw needn't show every extreme that they name: `cache_lengths`: the number of cached positions of each row; the new token stands at that position; some row holds exactly 1280.
All inputs are finite; a program needn't handle non-finite values.
Results may differ from the reference program's by a relative error of at most 0.02.
Values may be sent and summed in bfloat16 or wider, within the bound.
A program may use at most 128 MiB of HBM per device.

```python
import math
import jax
import jax.numpy as jnp
from jax import lax

D = 5120
HD = 128
QH = 20
KVH = 4
CACHE = 1280
ROWS = 512
QW = 2560
KVW = 512


def draw_hidden_in(key, part):
    key = jax.random.fold_in(key, 11)
    row_key, column_key_part, base_key = jax.random.split(key, 3)
    row_scale_factors = jnp.exp(jax.random.uniform(row_key, (ROWS, 1), jnp.float32, math.log(0.3), math.log(3.0)))
    ramp = jnp.sqrt(1.0 + 2.0 * jnp.arange(D, dtype=jnp.float32) / (D - 1))
    col_scales = jnp.exp(jax.random.uniform(column_key_part, (1, D), jnp.float32, math.log(0.4), math.log(2.5))) * ramp[None, :]
    base_values = jnp.clip(jax.random.normal(base_key, (ROWS, D), jnp.float32), -5.0, 5.0)
    return (base_values * row_scale_factors * col_scales).astype(jnp.bfloat16)


def draw_cache_lengths(key, part):
    key = jax.random.fold_in(key, 31)
    length_key, pick_key = jax.random.split(key)
    lengths = jax.random.randint(length_key, (ROWS,), CACHE // 8, CACHE + 1, jnp.int32)
    chosen = jax.random.randint(pick_key, (), 0, ROWS, jnp.int32)
    return jnp.where(jnp.arange(ROWS, dtype=jnp.int32) == chosen, CACHE, lengths).astype(jnp.int32)


def draw_key_cache(key, part):
    key = jax.random.fold_in(key, 21)
    base_key = jax.random.fold_in(key, 0)
    cache_shape = (ROWS, KVH, CACHE, HD)
    base_values = jnp.clip(jax.random.normal(base_key, cache_shape, jnp.float32), -6.0, 6.0)
    return base_values.astype(jnp.bfloat16)


def shared_center(key):
    return 0.63 * jnp.clip(jax.random.normal(key, (KVH, HD), jnp.float32), -5.0, 5.0)


def draw_b_query(key, part):
    center = shared_center(key)
    key = jax.random.fold_in(key, 41)
    spread_values = 0.3 * jnp.clip(jax.random.normal(key, (KVH, QH // KVH, HD), jnp.float32), -5.0, 5.0)
    return (center[:, None, :] + spread_values).reshape(QH * HD).astype(jnp.float32)


def draw_b_key(key, part):
    center = shared_center(key)
    key = jax.random.fold_in(key, 51)
    spread_values = 0.2 * jnp.clip(jax.random.normal(key, (KVH, HD), jnp.float32), -5.0, 5.0)
    return (center + spread_values).reshape(KVH * HD).astype(jnp.float32)


def strengthened(array, key, source, target, blocks, factor):
    owner, partner = [(jnp.arange(array.shape[dim]) // (array.shape[dim] // blocks)).reshape([-1 if axis == dim else 1 for axis in range(array.ndim)]) for dim in (source, target)]
    chosen = jax.random.permutation(key, blocks)[partner]
    strong = (owner == chosen) | (owner == (partner + blocks // 2) % blocks)
    return jnp.where(strong, factor * array, array)


def steps_of(stream_key, extent, shards, least, largest):
    def one(position, parts):
        draws = jax.random.uniform(jax.random.fold_in(jax.random.fold_in(stream_key, 6), position), (parts,), jnp.float32, least / len(shards), largest / len(shards))
        return jnp.repeat(jnp.exp(draws), extent[position] // parts).reshape((-1,) + (1,) * (len(extent) - position - 1))

    gain = one(*shards[0])
    for cut in shards[1:]:
        gain = gain * one(*cut)
    return gain


def bell_draw(key, dims, width, most, shards=(), kind=jnp.bfloat16):
    result = jax.random.normal(key, dims, jnp.float32) * width
    if len(shards) > 0:
        result = steps_of(key, dims, shards, -0.22, 0.18) * result
    return jnp.clip(result, min=-most, max=most).astype(kind)


def gaussian_with(stream_key, dims, deviation, reach, pieces, heavy, kind=jnp.bfloat16):
    drawn = deviation * jax.random.normal(stream_key, dims, jnp.float32)
    if pieces:
        drawn = drawn * steps_of(stream_key, dims, pieces, -0.22, 0.18)
    return jnp.clip(strengthened(drawn, jax.random.fold_in(stream_key, 3), *heavy), -reach, reach).astype(kind)


def setup_inputs(seed: int = 0) -> dict:
    streams_of = jax.random.split(jax.random.key(seed), 14)
    return {
        "hidden_in": draw_hidden_in(jax.random.fold_in(streams_of[13], 71), 0),
        "cache_lengths": draw_cache_lengths(jax.random.fold_in(streams_of[13], 71), 0),
        "in_gain": jnp.clip(1.0 + 0.18 * jax.random.normal(streams_of[2], (D,), jnp.float32), 0.1, 1.9),
        "post_gain": jnp.clip(1.0 + 0.18 * jax.random.normal(streams_of[3], (D,), jnp.float32), 0.1, 1.9),
        "w_query": bell_draw(streams_of[4], (D, QW), D ** -0.5, 0.078125, ((1, 4),)),
        "b_query": draw_b_query(jax.random.fold_in(streams_of[13], 71), 0),
        "b_key": draw_b_key(jax.random.fold_in(streams_of[13], 71), 0),
        "b_value": bell_draw(streams_of[7], (KVW,), 0.5, 3.0, ((0, 4),), jnp.float32),
        "w_out": gaussian_with(streams_of[8], (QW, D), HD ** -0.5, 0.75, ((0, 4),), (0, 1, 4, 2.0)),
        "key_cache": draw_key_cache(jax.random.fold_in(streams_of[13], 71), 0),
        "value_cache": bell_draw(streams_of[10], (ROWS, KVH, CACHE, HD), 1.0, 6.0, ((0, 32), (1, 4))),
        "next_key_weight": bell_draw(streams_of[11], (D, KVW), D ** -0.5, 0.078125, ((0, 128),)),
        "next_w_value": bell_draw(streams_of[12], (D, KVW), D ** -0.5, 0.078125, ((0, 128),)),
    }


NORM_EPS = 1e-06
ROPE_BASE = 1000000.0

def rotate_heads(vectors, positions):
    half_width = vectors.shape[-1] // 2
    exponent = jnp.arange(half_width, dtype=jnp.float32) * (-2.0 / vectors.shape[-1])
    frequency = jnp.power(ROPE_BASE, exponent)
    rotary_angles = positions.astype(jnp.float32)[:, None] * frequency[None, :]
    cosine = jnp.cos(rotary_angles)[:, None, :]
    sine_part = jnp.sin(rotary_angles)[:, None, :]
    first_half = vectors[..., :half_width]
    second_half = vectors[..., half_width:]
    return jnp.concatenate([first_half * cosine - second_half * sine_part, second_half * cosine + first_half * sine_part], axis=-1)

def reference(hidden_in, cache_lengths, in_gain, post_gain, w_query, b_query, b_key, b_value, w_out, key_cache, value_cache, next_key_weight, next_w_value):
    rows_f32 = hidden_in.astype(jnp.float32)
    inverse_in = lax.rsqrt(lax.optimization_barrier(jnp.mean(rows_f32 * rows_f32, axis=-1, keepdims=True)) + NORM_EPS)
    normed_in = (rows_f32 * inverse_in * in_gain).astype(jnp.bfloat16)
    query_raw = jnp.dot(normed_in, w_query, preferred_element_type=jnp.float32) + b_query
    key_raw = jnp.dot(normed_in, next_key_weight, preferred_element_type=jnp.float32) + b_key
    value_raw = jnp.dot(normed_in, next_w_value, preferred_element_type=jnp.float32) + b_value
    queries = rotate_heads(query_raw.reshape(ROWS, QH, HD), cache_lengths).astype(jnp.bfloat16)
    fresh_key = rotate_heads(key_raw.reshape(ROWS, KVH, HD), cache_lengths).astype(jnp.bfloat16)
    new_value = value_raw.reshape(ROWS, KVH, HD).astype(jnp.bfloat16)
    per_group = QH // KVH
    score_scale = HD ** (-0.5)

    def attend_row(items):
        query_row, keys_row, value_rows, length_row, own_key, own_value = items
        grouped_heads = query_row.reshape(KVH, per_group, HD).astype(jnp.float32)
        scores = jnp.einsum('kgd,kjd->kgj', grouped_heads, keys_row.astype(jnp.float32)) * score_scale
        own_score = jnp.einsum('kgd,kd->kg', grouped_heads, own_key.astype(jnp.float32)) * score_scale
        in_cache = (jnp.arange(CACHE, dtype=jnp.int32) < length_row)[None, None, :]
        peak_score = jnp.maximum(lax.optimization_barrier(jnp.max(jnp.where(in_cache, scores, -jnp.inf), axis=-1)), own_score)
        weights = jnp.where(in_cache, jnp.exp(scores - peak_score[..., None]), 0.0)
        own_weight = jnp.exp(own_score - peak_score)
        denominator = lax.optimization_barrier(jnp.sum(weights, axis=-1)) + own_weight
        probs = (weights / denominator[..., None]).astype(jnp.bfloat16)
        own_prob = (own_weight / denominator).astype(jnp.bfloat16)
        mixed = jnp.einsum('kgj,kjd->kgd', probs.astype(jnp.float32), value_rows.astype(jnp.float32))
        mixed = mixed + own_prob.astype(jnp.float32)[..., None] * own_value.astype(jnp.float32)[:, None, :]
        return mixed.astype(jnp.bfloat16).reshape(QH * HD)
    context = lax.map(attend_row, (queries, key_cache, value_cache, cache_lengths, fresh_key, new_value))
    attended = jnp.dot(context, w_out, preferred_element_type=jnp.float32).astype(jnp.bfloat16)
    residual = (rows_f32 + attended.astype(jnp.float32)).astype(jnp.bfloat16)
    resid_f32 = residual.astype(jnp.float32)
    inverse_post = lax.rsqrt(lax.optimization_barrier(jnp.mean(resid_f32 * resid_f32, axis=-1, keepdims=True)) + NORM_EPS)
    normed = (resid_f32 * inverse_post * post_gain).astype(jnp.bfloat16)
    return (attended, normed, next_key_weight, next_w_value)
```

```python
import functools
import math

import jax
import jax.numpy as jnp
from jax import lax
from jax.experimental import pallas as pl
from jax.experimental.pallas import tpu as pltpu
from jax.sharding import PartitionSpec as P

MESH = pl.DeviceIdType.MESH
F32 = jnp.float32
BF16 = jnp.bfloat16

D = 5120
HD = 128
ROWS = 16
HEADS = 5
CACHE = 1280
WIDTH = 1280
SHARD = 40
BLOCK = 160
CHUNK = 640
CHUNKS = 8
EPS = 1e-06
ROPE_BASE = 1000000.0
SCALE = HD ** (-0.5)

HIDDEN = 0
LINE = 3
GATHER = 17
SHARE = 57
STAT = 60
COPIES = 63
L_HID, L_LEN, L_IN, L_POST, L_BQ, L_BK, L_BV, L_OWNK, L_OWNV = range(9)
L_WQ = 9
L_KC = L_WQ + CHUNKS
L_VC = L_KC + 8
L_WO = L_VC + 8
LOCALS = L_WO + 4


def kernel(
    hid, lens, in_gain, post_gain, wq, bq, bk, bv, wo, kc, vc, nk, nv,
    att_out, norm_out, k_out, v_out,
    h_buf, len_s, ig, pg, bq_s, bk_s, bv_s, x_buf, wq_s, kc_s, vc_s, wo_s,
    n_buf, q_s, o_s, m_s, l_s, ctx_s, send_buf, r_buf, stat_send, stat_buf,
    lsem, ssem, rsem,
):
    g = lax.axis_index("grp")
    t = lax.axis_index("tp")
    xh, z, y = g // 16, (g // 4) % 4, g % 4

    def group(xh_, z_, y_):
        return xh_ * 16 + z_ * 4 + y_

    def local(src, dst, i):
        return pltpu.make_async_copy(src, dst, lsem.at[i])

    def remote(src, dst, i, dev):
        return pltpu.make_async_remote_copy(
            src_ref=src, dst_ref=dst, send_sem=ssem.at[i], recv_sem=rsem.at[i], device_id=dev, device_id_type=MESH
        )

    columns = pl.ds(pl.multiple_of(t * HD, HD), HD)
    local(hid, h_buf.at[t], L_HID).start()
    local(nk.at[:, columns], x_buf.at[0, xh, t], L_OWNK).start()
    local(nv.at[:, columns], x_buf.at[1, xh, t], L_OWNV).start()
    small = [
        local(lens, len_s, L_LEN),
        local(in_gain, ig, L_IN),
        local(post_gain, pg, L_POST),
        local(bq, bq_s, L_BQ),
        local(bk, bk_s, L_BK),
        local(bv, bv_s, L_BV),
    ]
    for c in small:
        c.start()

    line = [(dx, dt) for dx in (0, 1) for dt in range(4) if (dx, dt) != (0, 0)]
    barrier = pltpu.get_barrier_semaphore()
    partners = [(group((xh + dx) % 2, z, y), (t + dt) % 4) for dx, dt in line]
    partners += [(group(xh, z, (y + d) % 4), t) for d in (1, 3)]
    partners += [(group(xh, (z + d) % 4, y), t) for d in (1, 3)]
    for dev in partners:
        pl.semaphore_signal(barrier, inc=1, device_id=dev, device_id_type=MESH)

    def wq_copy(i):
        return local(wq.at[pl.ds(i * CHUNK, CHUNK)], wq_s.at[i], L_WQ + i)

    def kc_copy(p):
        return local(kc.at[pl.ds(2 * p, 2)], kc_s.at[pl.ds(2 * p, 2)], L_KC + p)

    def vc_copy(p):
        return local(vc.at[pl.ds(2 * p, 2)], vc_s.at[pl.ds(2 * p, 2)], L_VC + p)

    def wo_copy(i):
        return local(wo.at[:, pl.ds(pl.multiple_of(i * WIDTH, WIDTH), WIDTH)], wo_s.at[i], L_WO + i)

    pl.semaphore_wait(barrier, len(partners))

    line_copies = []
    for n, (dx, dt) in enumerate(line):
        to_t = (t + dt) % 4
        dev = (group((xh + dx) % 2, z, y), to_t)
        cols = pl.ds(pl.multiple_of(to_t * HD, HD), HD)
        for kv, src in ((0, nk), (1, nv)):
            c = remote(src.at[:, cols], x_buf.at[kv, xh, t], LINE + 2 * n + kv, dev)
            c.start()
            line_copies.append(c)
    hidden_copies = []
    for dt in (1, 2, 3):
        c = remote(hid, h_buf.at[t], HIDDEN + dt - 1, (g, (t + dt) % 4))
        c.start()
        hidden_copies.append(c)

    def start_all(make, count):
        def body(i, _):
            make(i).start()
            return 0

        lax.fori_loop(0, count, body, 0)

    start_all(wq_copy, CHUNKS)
    start_all(kc_copy, 8)
    start_all(vc_copy, 8)
    start_all(wo_copy, 4)

    for c in small:
        c.wait()
    row_ids = lax.broadcasted_iota(jnp.int32, (ROWS, HD), 0)
    lane_ids = lax.broadcasted_iota(jnp.int32, (ROWS, HD), 1)
    position = jnp.zeros((ROWS, HD), jnp.int32)
    for r in range(ROWS):
        position = jnp.where(row_ids == r, len_s[r], position)
    exponent = (lane_ids % (HD // 2)).astype(F32) * (-2.0 / HD * math.log(ROPE_BASE))
    angle = position.astype(F32) * jnp.exp(exponent)
    cosine = jnp.cos(angle)
    sine = jnp.where(lane_ids < HD // 2, -jnp.sin(angle), jnp.sin(angle))

    def rotate(v):
        return v * cosine + pltpu.roll(v, HD // 2, 1) * sine

    local(nk.at[:, columns], x_buf.at[0, xh, t], L_OWNK).wait()
    local(nv.at[:, columns], x_buf.at[1, xh, t], L_OWNV).wait()
    for n, (dx, dt) in enumerate(line):
        for kv, src in ((0, nk), (1, nv)):
            land = x_buf.at[kv, (xh - dx + 2) % 2, (t - dt + 4) % 4]
            remote(src.at[:, columns], land, LINE + 2 * n + kv, (g, t)).wait_recv()
    for kv, out in ((0, k_out), (1, v_out)):
        for i in (0, 1):
            out[i, z, y] = x_buf[kv, i].astype(F32).reshape(BLOCK, HD).astype(BF16)

    class Gather:
        def __init__(self, buf, first, second, at, base):
            self.buf, self.a, self.b, self.at, self.base = buf, first, second, at, base
            self.started = []

        def slot(self, da, db, half=None):
            p, q = (self.a + da + 4) % 4, (self.b + db + 4) % 4
            zz, yy = self.at(p, q)
            return self.buf.at[slice(None) if half is None else half, zz, yy]

        def dev(self, da, db):
            zz, yy = self.at((self.a + da + 4) % 4, (self.b + db + 4) % 4)
            return (group(xh, zz, yy), t)

        def send(self, src, i, da, db):
            c = remote(src, src, self.base + i, self.dev(da, db))
            c.start()
            self.started.append(c)

        def recv(self, land, i):
            remote(land, land, self.base + i, (g, t)).wait_recv()

        def first_own(self):
            self.send(self.slot(0, 0), 0, 1, 0)
            self.send(self.slot(0, 0), 1, -1, 0)

        def first_forward(self):
            self.recv(self.slot(-1, 0), 0)
            self.send(self.slot(-1, 0, 0), 2, 1, 0)
            self.recv(self.slot(1, 0), 1)
            self.send(self.slot(1, 0, 1), 3, -1, 0)

        def first_far(self):
            self.recv(self.slot(2, 0, 0), 2)
            self.recv(self.slot(2, 0, 1), 3)

        def second(self, s):
            self.send(self.slot(s, 0), 4 + 4 * (s % 4), 0, 1)
            self.send(self.slot(s, 0), 5 + 4 * (s % 4), 0, -1)

        def second_forward(self, s):
            i = 4 + 4 * (s % 4)
            self.recv(self.slot(s, -1), i)
            self.send(self.slot(s, -1, 0), i + 2, 0, 1)
            self.recv(self.slot(s, 1), i + 1)
            self.send(self.slot(s, 1, 1), i + 3, 0, -1)

        def second_far(self, s):
            i = 4 + 4 * (s % 4)
            self.recv(self.slot(s, 2, 0), i + 2)
            self.recv(self.slot(s, 2, 1), i + 3)

    keys = Gather(k_out, y, z, lambda p, q: (q, p), GATHER)
    values = Gather(v_out, z, y, lambda p, q: (p, q), GATHER + 20)
    both = (keys, values)
    for w in both:
        w.first_own()
    for w in both:
        w.second(0)

    local(hid, h_buf.at[t], L_HID).wait()
    for dt in (1, 2, 3):
        remote(hid, h_buf.at[(t - dt + 4) % 4], HIDDEN + dt - 1, (g, t)).wait_recv()
    squares = jnp.zeros((ROWS, HD), F32)
    for i in range(4):
        for j in range(WIDTH // HD):
            v = h_buf[i, :, j * HD : (j + 1) * HD].astype(F32)
            squares = squares + v * v
    inverse = lax.rsqrt(jnp.sum(squares, axis=1, keepdims=True) * (1.0 / D) + EPS)
    for i in range(CHUNKS):
        for j in range(CHUNK // HD):
            c = (i % 2) * (CHUNK // HD) + j
            v = h_buf[i // 2, :, c * HD : (c + 1) * HD].astype(F32)
            k = i * (CHUNK // HD) + j
            n_buf[i, :, j * HD : (j + 1) * HD] = (v * inverse * ig[k : k + 1, :]).astype(BF16)

    for w in both:
        w.first_forward()
    for w in both:
        w.second(-1)
    for w in both:
        w.second(1)

    def query_step(i, total):
        wq_copy(i).wait()
        return total + jnp.dot(n_buf[i], wq_s[i], preferred_element_type=F32)

    total = lax.fori_loop(0, CHUNKS // 2, query_step, jnp.zeros((ROWS, HEADS * HD), F32))
    for w in both:
        w.second_forward(0)
    for w in both:
        w.first_far()
    for w in both:
        w.second(2)
    total = lax.fori_loop(CHUNKS // 2, CHUNKS, query_step, total)

    q_s[...] = jnp.zeros_like(q_s)
    for h in range(HEADS):
        v = rotate(total[:, h * HD : (h + 1) * HD] + bq_s[h : h + 1, :])
        q_s[:, h, :] = v.astype(BF16).astype(F32)

    upper = lax.broadcasted_iota(jnp.int32, (16, 1), 0) < 8
    slot_ids = lax.broadcasted_iota(jnp.int32, (16, CACHE), 1)

    def attend(p, _):
        kc_copy(p).wait()
        vc_copy(p).wait()
        q2 = q_s[pl.ds(2 * p, 2)].reshape(16, HD)
        left = jnp.concatenate([jnp.where(upper, q2, 0.0), jnp.where(upper, 0.0, q2)], axis=1).astype(BF16)
        right = jnp.concatenate([kc_s[2 * p], kc_s[2 * p + 1]], axis=1)
        scores = lax.dot_general(left, right, (((1,), (1,)), ((), ())), preferred_element_type=F32) * SCALE
        length = jnp.where(upper, len_s[2 * p], len_s[2 * p + 1])
        scores = jnp.where(slot_ids < length, scores, -jnp.inf)
        peak = jnp.max(scores, axis=1, keepdims=True)
        weights = jnp.exp(scores - peak)
        total_weight = jnp.sum(weights, axis=1, keepdims=True)
        mixed = jnp.dot(
            weights.astype(BF16), jnp.concatenate([vc_s[2 * p], vc_s[2 * p + 1]], axis=1), preferred_element_type=F32
        )
        rows = pl.ds(2 * p, 2)
        o_s[rows] = jnp.where(upper, mixed[:, :HD], mixed[:, HD:]).reshape(2, 8, HD)
        m_s[rows] = jnp.broadcast_to(peak, (16, HD)).reshape(2, 8, HD)
        l_s[rows] = jnp.broadcast_to(total_weight, (16, HD)).reshape(2, 8, HD)
        return 0

    lax.fori_loop(0, 2, attend, 0)
    for w in both:
        w.second_forward(-1)
    lax.fori_loop(2, 4, attend, 0)
    for w in both:
        w.second_forward(1)
    lax.fori_loop(4, 6, attend, 0)
    for w in both:
        w.second_forward(2)
    lax.fori_loop(6, 8, attend, 0)
    for s in (0, -1, 1, 2):
        for w in both:
            w.second_far(s)

    def own_step(i, sums):
        x = n_buf[i]
        a, b = i // 4, i % 4
        return tuple(
            s + jnp.dot(x, out[a, b].reshape(CHUNK, HD), preferred_element_type=F32)
            for s, out in zip(sums, (k_out, v_out))
        )

    zero = jnp.zeros((ROWS, HD), F32)
    key_raw, value_raw = lax.fori_loop(0, CHUNKS, own_step, (zero, zero))
    new_key = rotate(key_raw + bk_s[...]).astype(BF16).astype(F32)
    new_value = (value_raw + bv_s[...]).astype(BF16).astype(F32)
    for h in range(HEADS):
        own_score = jnp.sum(q_s[:, h, :] * new_key, axis=1, keepdims=True) * SCALE
        peak = m_s[:, h, :]
        top = jnp.maximum(peak, own_score)
        a = jnp.exp(peak - top)
        b = jnp.exp(own_score - top)
        denominator = a * l_s[:, h, :] + b
        ctx_s[:, h * HD : (h + 1) * HD] = ((a * o_s[:, h, :] + b * new_value) / denominator).astype(BF16)

    for i in range(4):
        wo_copy(i).wait()
    share_copies = []
    for n, dt in enumerate((2, 1, 3)):
        to_t = (t + dt) % 4
        part = jnp.dot(ctx_s[...], wo_s[to_t], preferred_element_type=F32)
        send_buf[dt - 1] = part.astype(BF16)
        c = remote(send_buf.at[dt - 1], r_buf.at[dt - 1], SHARE + dt - 1, (g, to_t))
        c.start()
        share_copies.append(c)
    share = jnp.dot(ctx_s[...], wo_s[t], preferred_element_type=F32)
    for dt in (2, 1, 3):
        remote(send_buf.at[dt - 1], r_buf.at[dt - 1], SHARE + dt - 1, (g, t)).wait_recv()
    for i in range(3):
        share = share + r_buf[i].astype(F32)
    attended = share.astype(BF16)
    att_out[...] = attended
    residual = (h_buf[t].astype(F32) + attended.astype(F32)).astype(BF16).astype(F32)
    own_squares = jnp.sum(residual * residual, axis=1, keepdims=True)
    stat_send[...] = jnp.broadcast_to(own_squares, (ROWS, HD))
    stat_copies = []
    for dt in (1, 2, 3):
        c = remote(stat_send, stat_buf.at[dt - 1], STAT + dt - 1, (g, (t + dt) % 4))
        c.start()
        stat_copies.append(c)
    for dt in (1, 2, 3):
        remote(stat_send, stat_buf.at[dt - 1], STAT + dt - 1, (g, t)).wait_recv()
    square_total = own_squares + stat_buf[0] + stat_buf[1] + stat_buf[2]
    inverse_post = lax.rsqrt(square_total * (1.0 / D) + EPS)
    for j in range(WIDTH // HD):
        gain = pg[pl.ds(t * (WIDTH // HD) + j, 1), :]
        norm_out[:, j * HD : (j + 1) * HD] = (residual[:, j * HD : (j + 1) * HD] * inverse_post * gain).astype(BF16)

    for c in line_copies + hidden_copies + keys.started + values.started + share_copies + stat_copies:
        c.wait_send()


def shards(
    hidden_in, cache_lengths, in_gain, post_gain, w_query, b_query, b_key, b_value, w_out,
    key_cache, value_cache, next_key_weight, next_w_value,
):
    hbm = pl.BlockSpec(memory_space=pltpu.HBM)
    vmem = pl.BlockSpec(memory_space=pltpu.VMEM)
    attended, normed, key_out, value_out = pl.pallas_call(
        kernel,
        out_shape=[
            pltpu.VMEM((ROWS, WIDTH), BF16),
            pltpu.VMEM((ROWS, WIDTH), BF16),
            pltpu.VMEM((2, 4, 4, BLOCK, HD), BF16),
            pltpu.VMEM((2, 4, 4, BLOCK, HD), BF16),
        ],
        in_specs=[hbm] * 13,
        out_specs=[vmem] * 4,
        scratch_shapes=[
            pltpu.VMEM((4, ROWS, WIDTH), BF16),
            pltpu.SMEM((ROWS,), jnp.int32),
            pltpu.VMEM((D // HD, HD), F32),
            pltpu.VMEM((D // HD, HD), F32),
            pltpu.VMEM((HEADS, HD), F32),
            pltpu.VMEM((1, HD), F32),
            pltpu.VMEM((1, HD), F32),
            pltpu.VMEM((2, 2, 4, SHARD, HD), BF16),
            pltpu.VMEM((CHUNKS, CHUNK, HEADS * HD), BF16),
            pltpu.VMEM((ROWS, CACHE, HD), BF16),
            pltpu.VMEM((ROWS, CACHE, HD), BF16),
            pltpu.VMEM((4, HEADS * HD, WIDTH), BF16),
            pltpu.VMEM((CHUNKS, ROWS, CHUNK), BF16),
            pltpu.VMEM((ROWS, 8, HD), F32),
            pltpu.VMEM((ROWS, 8, HD), F32),
            pltpu.VMEM((ROWS, 8, HD), F32),
            pltpu.VMEM((ROWS, 8, HD), F32),
            pltpu.VMEM((ROWS, HEADS * HD), BF16),
            pltpu.VMEM((3, ROWS, WIDTH), BF16),
            pltpu.VMEM((3, ROWS, WIDTH), BF16),
            pltpu.VMEM((ROWS, HD), F32),
            pltpu.VMEM((3, ROWS, HD), F32),
            pltpu.SemaphoreType.DMA((LOCALS,)),
            pltpu.SemaphoreType.DMA((COPIES,)),
            pltpu.SemaphoreType.DMA((COPIES,)),
        ],
        compiler_params=pltpu.CompilerParams(
            collective_id=0, has_side_effects=True, vmem_limit_bytes=48 * 1024 * 1024
        ),
        name="decode",
    )(
        hidden_in,
        cache_lengths,
        in_gain.reshape(D // HD, HD),
        post_gain.reshape(D // HD, HD),
        w_query,
        b_query.reshape(HEADS, HD),
        b_key.reshape(1, HD),
        b_value.reshape(1, HD),
        w_out,
        key_cache.reshape(ROWS, CACHE, HD),
        value_cache.reshape(ROWS, CACHE, HD),
        next_key_weight,
        next_w_value,
    )
    return attended, normed, key_out.reshape(D, HD), value_out.reshape(D, HD)


def solution(mesh):
    in_specs = (
        P("grp", "tp"),
        P("grp"),
        P(),
        P(),
        P(None, "tp"),
        P("tp"),
        P("tp"),
        P("tp"),
        P("tp", None),
        P("grp", "tp", None, None),
        P("grp", "tp", None, None),
        P(("grp", "tp"), None),
        P(("grp", "tp"), None),
    )
    out_specs = (P("grp", "tp"), P("grp", "tp"), P(None, "tp"), P(None, "tp"))
    return jax.shard_map(shards, mesh=mesh, in_specs=in_specs, out_specs=out_specs, check_vma=False)
```

```python
import functools
import math

import jax
import jax.numpy as jnp
from jax import lax
from jax.experimental import pallas as pl
from jax.experimental.pallas import tpu as pltpu
from jax.sharding import PartitionSpec as P

MESH = pl.DeviceIdType.MESH
F32 = jnp.float32
BF16 = jnp.bfloat16

D = 5120
HD = 128
ROWS = 16
HEADS = 5
CACHE = 1280
WIDTH = 1280
SHARD = 40
BLOCK = 160
CHUNK = 640
CHUNKS = 8
EPS = 1e-06
ROPE_BASE = 1000000.0
SCALE = HD ** (-0.5)

HIDDEN = 0
LINE = 3
GATHER = 17
SHARE = 57
STAT = 60
SLICE = 63
PARTIAL = 69
COPIES = 75
L_HID, L_LEN, L_IN, L_POST, L_BQ, L_BK, L_BV, L_OWNK, L_OWNV = range(9)
L_WQ = 9
L_KC = L_WQ + CHUNKS
L_VC = L_KC + 8
L_WO = L_VC + 8
LOCALS = L_WO + 4


def kernel(
    hid, lens, in_gain, post_gain, wq, bq, bk, bv, wo, kc, vc, nk, nv,
    att_out, norm_out, k_out, v_out,
    h_buf, len_s, ig, pg, bq_s, bk_s, bv_s, x_buf, wq_s, kc_s, vc_s, wo_s,
    n_buf, n2_buf, nz_buf, ny_buf, pk_send, pv_send, pk_buf, pv_buf,
    q_s, o_s, m_s, l_s, ctx_s, send_buf, r_buf, stat_send, stat_buf,
    lsem, ssem, rsem,
):
    g = lax.axis_index("grp")
    t = lax.axis_index("tp")
    xh, z, y = g // 16, (g // 4) % 4, g % 4

    def group(xh_, z_, y_):
        return xh_ * 16 + z_ * 4 + y_

    def local(src, dst, i):
        return pltpu.make_async_copy(src, dst, lsem.at[i])

    def remote(src, dst, i, dev):
        return pltpu.make_async_remote_copy(
            src_ref=src, dst_ref=dst, send_sem=ssem.at[i], recv_sem=rsem.at[i], device_id=dev, device_id_type=MESH
        )

    columns = pl.ds(pl.multiple_of(t * HD, HD), HD)
    local(hid, h_buf.at[t], L_HID).start()
    local(nk.at[:, columns], x_buf.at[0, xh, t], L_OWNK).start()
    local(nv.at[:, columns], x_buf.at[1, xh, t], L_OWNV).start()
    small = [
        local(lens, len_s, L_LEN),
        local(in_gain, ig, L_IN),
        local(post_gain, pg, L_POST),
        local(bq, bq_s, L_BQ),
        local(bk, bk_s, L_BK),
        local(bv, bv_s, L_BV),
    ]
    for c in small:
        c.start()

    line = [(dx, dt) for dx in (0, 1) for dt in range(4) if (dx, dt) != (0, 0)]
    barrier = pltpu.get_barrier_semaphore()
    partners = [(group((xh + dx) % 2, z, y), (t + dt) % 4) for dx, dt in line]
    partners += [(group(xh, z, (y + d) % 4), t) for d in (1, 2, 3)]
    partners += [(group(xh, (z + d) % 4, y), t) for d in (1, 2, 3)]
    for dev in partners:
        pl.semaphore_signal(barrier, inc=1, device_id=dev, device_id_type=MESH)

    def wq_copy(i):
        return local(wq.at[pl.ds(i * CHUNK, CHUNK)], wq_s.at[i], L_WQ + i)

    def kc_copy(p):
        return local(kc.at[pl.ds(2 * p, 2)], kc_s.at[pl.ds(2 * p, 2)], L_KC + p)

    def vc_copy(p):
        return local(vc.at[pl.ds(2 * p, 2)], vc_s.at[pl.ds(2 * p, 2)], L_VC + p)

    def wo_copy(i):
        return local(wo.at[:, pl.ds(pl.multiple_of(i * WIDTH, WIDTH), WIDTH)], wo_s.at[i], L_WO + i)

    pl.semaphore_wait(barrier, len(partners))

    far_t, twin_t = (t + 2) % 4, t + 1 - 2 * (t % 2)
    far_twin = (twin_t + 2) % 4
    hidden_copies = [
        remote(hid, h_buf.at[t], HIDDEN, (g, far_t)),
        remote(hid, h_buf.at[t], HIDDEN + 1, (g, twin_t)),
    ]
    for c in hidden_copies:
        c.start()
    line_copies = []
    for n, (dx, dt) in enumerate(line):
        to_t = (t + dt) % 4
        dev = (group((xh + dx) % 2, z, y), to_t)
        cols = pl.ds(pl.multiple_of(to_t * HD, HD), HD)
        for kv, src in ((0, nk), (1, nv)):
            c = remote(src.at[:, cols], x_buf.at[kv, xh, t], LINE + 2 * n + kv, dev)
            c.start()
            line_copies.append(c)
    def start_all(make, count):
        def body(i, _):
            make(i).start()
            return 0

        lax.fori_loop(0, count, body, 0)

    start_all(wq_copy, CHUNKS)
    start_all(kc_copy, 8)
    start_all(vc_copy, 8)
    start_all(wo_copy, 4)

    for c in small:
        c.wait()
    row_ids = lax.broadcasted_iota(jnp.int32, (ROWS, HD), 0)
    lane_ids = lax.broadcasted_iota(jnp.int32, (ROWS, HD), 1)
    position = jnp.zeros((ROWS, HD), jnp.int32)
    for r in range(ROWS):
        position = jnp.where(row_ids == r, len_s[r], position)
    exponent = (lane_ids % (HD // 2)).astype(F32) * (-2.0 / HD * math.log(ROPE_BASE))
    angle = position.astype(F32) * jnp.exp(exponent)
    cosine = jnp.cos(angle)
    sine = jnp.where(lane_ids < HD // 2, -jnp.sin(angle), jnp.sin(angle))

    def rotate(v):
        return v * cosine + pltpu.roll(v, HD // 2, 1) * sine

    local(hid, h_buf.at[t], L_HID).wait()
    remote(hid, h_buf.at[far_t], HIDDEN, (g, t)).wait_recv()
    relay = remote(h_buf.at[far_t], h_buf.at[far_t], HIDDEN + 2, (g, twin_t))
    relay.start()
    hidden_copies.append(relay)
    remote(hid, h_buf.at[twin_t], HIDDEN + 1, (g, t)).wait_recv()
    remote(hid, h_buf.at[far_twin], HIDDEN + 2, (g, t)).wait_recv()
    squares = jnp.zeros((ROWS, HD), F32)
    for i in range(4):
        for j in range(WIDTH // HD):
            v = h_buf[i, :, j * HD : (j + 1) * HD].astype(F32)
            squares = squares + v * v
    inverse = lax.rsqrt(jnp.sum(squares, axis=1, keepdims=True) * (1.0 / D) + EPS)
    for i in range(CHUNKS):
        for j in range(CHUNK // HD):
            c = (i % 2) * (CHUNK // HD) + j
            v = h_buf[i // 2, :, c * HD : (c + 1) * HD].astype(F32)
            k = i * (CHUNK // HD) + j
            n_buf[i // 4, i % 4, :, j * HD : (j + 1) * HD] = (v * inverse * ig[k : k + 1, :]).astype(BF16)

    for b in range(4):
        n2_buf[b] = jnp.concatenate(
            [n_buf[i // 4, i % 4, :, b * BLOCK : (b + 1) * BLOCK].astype(F32) for i in range(CHUNKS)], axis=1
        ).astype(BF16)
    nz_buf[z] = n_buf[:, z]
    ny_buf[y] = n2_buf[y]
    slice_copies = []
    for d in (1, 2, 3):
        zz, yy = (z + d) % 4, (y + d) % 4
        slice_copies.append(remote(n_buf.at[:, zz], nz_buf.at[z], SLICE + d - 1, (group(xh, zz, y), t)))
        slice_copies.append(remote(n2_buf.at[yy], ny_buf.at[y], SLICE + d + 2, (group(xh, z, yy), t)))
    for c in slice_copies:
        c.start()

    local(nk.at[:, columns], x_buf.at[0, xh, t], L_OWNK).wait()
    local(nv.at[:, columns], x_buf.at[1, xh, t], L_OWNV).wait()
    for n, (dx, dt) in enumerate(line):
        for kv, src in ((0, nk), (1, nv)):
            land = x_buf.at[kv, (xh - dx + 2) % 2, (t - dt + 4) % 4]
            remote(src.at[:, columns], land, LINE + 2 * n + kv, (g, t)).wait_recv()
    for kv, out in ((0, k_out), (1, v_out)):
        for i in (0, 1):
            out[i, z, y] = x_buf[kv, i].astype(F32).reshape(BLOCK, HD).astype(BF16)

    class Gather:
        def __init__(self, buf, first, second, at, base):
            self.buf, self.a, self.b, self.at, self.base = buf, first, second, at, base
            self.started = []

        def slot(self, da, db, half=None):
            p, q = (self.a + da + 4) % 4, (self.b + db + 4) % 4
            zz, yy = self.at(p, q)
            return self.buf.at[slice(None) if half is None else half, zz, yy]

        def dev(self, da, db):
            zz, yy = self.at((self.a + da + 4) % 4, (self.b + db + 4) % 4)
            return (group(xh, zz, yy), t)

        def send(self, src, i, da, db):
            c = remote(src, src, self.base + i, self.dev(da, db))
            c.start()
            self.started.append(c)

        def recv(self, land, i):
            remote(land, land, self.base + i, (g, t)).wait_recv()

        def first_own(self):
            for i, d in enumerate((1, -1, 2)):
                self.send(self.slot(0, 0), i, d, 0)

        def first_near(self):
            self.recv(self.slot(-1, 0), 0)
            self.recv(self.slot(1, 0), 1)

        def first_far(self):
            self.recv(self.slot(2, 0), 2)

        def second(self, s):
            self.send(self.slot(s, 0), 4 + 4 * (s % 4), 0, 1)
            self.send(self.slot(s, 0), 5 + 4 * (s % 4), 0, -1)

        def second_forward(self, s):
            i = 4 + 4 * (s % 4)
            self.recv(self.slot(s, -1), i)
            self.send(self.slot(s, -1, 0), i + 2, 0, 1)
            self.recv(self.slot(s, 1), i + 1)
            self.send(self.slot(s, 1, 1), i + 3, 0, -1)

        def second_far(self, s):
            i = 4 + 4 * (s % 4)
            self.recv(self.slot(s, 2, 0), i + 2)
            self.recv(self.slot(s, 2, 1), i + 3)

    keys = Gather(k_out, y, z, lambda p, q: (q, p), GATHER)
    values = Gather(v_out, z, y, lambda p, q: (p, q), GATHER + 20)
    both = (keys, values)
    for w in both:
        w.first_own()

    for i in range(CHUNKS):
        wq_copy(i).wait()
    total = jnp.dot(n_buf[0, 0], wq_s[0], preferred_element_type=F32)
    for i in range(1, CHUNKS):
        total = total + jnp.dot(n_buf[i // 4, i % 4], wq_s[i], preferred_element_type=F32)
    q_s[...] = jnp.zeros_like(q_s)
    for h in range(HEADS):
        v = rotate(total[:, h * HD : (h + 1) * HD] + bq_s[h : h + 1, :])
        q_s[:, h, :] = v.astype(BF16).astype(F32)

    for w in both:
        w.second(0)

    upper = lax.broadcasted_iota(jnp.int32, (16, 1), 0) < 8
    slot_ids = lax.broadcasted_iota(jnp.int32, (16, CACHE), 1)

    def attend(p):
        q2 = q_s[pl.ds(2 * p, 2)].reshape(16, HD)
        left = jnp.concatenate([jnp.where(upper, q2, 0.0), jnp.where(upper, 0.0, q2)], axis=1).astype(BF16)
        right = jnp.concatenate([kc_s[2 * p], kc_s[2 * p + 1]], axis=1)
        scores = lax.dot_general(left, right, (((1,), (1,)), ((), ())), preferred_element_type=F32) * SCALE
        length = jnp.where(upper, len_s[2 * p], len_s[2 * p + 1])
        scores = jnp.where(slot_ids < length, scores, -jnp.inf)
        peak = jnp.max(scores, axis=1, keepdims=True)
        weights = jnp.exp(scores - peak)
        total_weight = jnp.sum(weights, axis=1, keepdims=True)
        mixed = jnp.dot(
            weights.astype(BF16), jnp.concatenate([vc_s[2 * p], vc_s[2 * p + 1]], axis=1), preferred_element_type=F32
        )
        rows = pl.ds(2 * p, 2)
        o_s[rows] = jnp.where(upper, mixed[:, :HD], mixed[:, HD:]).reshape(2, 8, HD)
        m_s[rows] = jnp.broadcast_to(peak, (16, HD)).reshape(2, 8, HD)
        l_s[rows] = jnp.broadcast_to(total_weight, (16, HD)).reshape(2, 8, HD)

    def attend_twice(i, _):
        for p in (2 * i, 2 * i + 1):
            kc_copy(p).wait()
            vc_copy(p).wait()
        for p in (2 * i, 2 * i + 1):
            attend(p)
        return 0

    lax.fori_loop(0, 3, attend_twice, 0)
    for w in both:
        w.first_near()
    for w in both:
        w.second(-1)
    for w in both:
        w.second(1)

    for w in both:
        w.first_far()
    for d in (1, 2, 3):
        zz, yy = (z - d + 4) % 4, (y - d + 4) % 4
        remote(n_buf.at[:, z], nz_buf.at[zz], SLICE + d - 1, (g, t)).wait_recv()
        remote(n2_buf.at[y], ny_buf.at[yy], SLICE + d + 2, (g, t)).wait_recv()
    key_part = jnp.zeros((4 * ROWS, HD), F32)
    for i in (0, 1):
        key_part = key_part + jnp.dot(
            nz_buf[:, i].reshape(4 * ROWS, CHUNK), k_out[i, z].reshape(CHUNK, HD), preferred_element_type=F32
        )
    pk_send[...] = key_part.reshape(4, ROWS, HD)
    value_part = jnp.dot(
        ny_buf[...].reshape(4 * ROWS, 2 * CHUNK), v_out[:, :, y].reshape(2 * CHUNK, HD), preferred_element_type=F32
    )
    pv_send[...] = value_part.reshape(4, ROWS, HD)
    partial_copies = []
    for d in (1, 2, 3):
        zz, yy = (z + d) % 4, (y + d) % 4
        partial_copies.append(remote(pk_send.at[zz], pk_buf.at[d - 1], PARTIAL + d - 1, (group(xh, zz, y), t)))
        partial_copies.append(remote(pv_send.at[yy], pv_buf.at[d - 1], PARTIAL + d + 2, (group(xh, z, yy), t)))
    for c in partial_copies:
        c.start()
    for w in both:
        w.second(2)
    attend_twice(3, 0)
    for w in both:
        w.second_forward(0)

    for d in (1, 2, 3):
        remote(pk_send.at[z], pk_buf.at[d - 1], PARTIAL + d - 1, (g, t)).wait_recv()
        remote(pv_send.at[y], pv_buf.at[d - 1], PARTIAL + d + 2, (g, t)).wait_recv()
    key_raw = pk_send[z] + pk_buf[0] + pk_buf[1] + pk_buf[2]
    value_raw = pv_send[y] + pv_buf[0] + pv_buf[1] + pv_buf[2]
    new_key = rotate(key_raw + bk_s[...]).astype(BF16).astype(F32)
    new_value = (value_raw + bv_s[...]).astype(BF16).astype(F32)
    for h in range(HEADS):
        own_score = jnp.sum(q_s[:, h, :] * new_key, axis=1, keepdims=True) * SCALE
        peak = m_s[:, h, :]
        top = jnp.maximum(peak, own_score)
        a = jnp.exp(peak - top)
        b = jnp.exp(own_score - top)
        denominator = a * l_s[:, h, :] + b
        ctx_s[:, h * HD : (h + 1) * HD] = ((a * o_s[:, h, :] + b * new_value) / denominator).astype(BF16)

    for i in range(4):
        wo_copy(i).wait()
    share_copies = []
    for n, dt in enumerate((2, 1, 3)):
        to_t = (t + dt) % 4
        part = jnp.dot(ctx_s[...], wo_s[to_t], preferred_element_type=F32)
        send_buf[dt - 1] = part.astype(BF16)
        c = remote(send_buf.at[dt - 1], r_buf.at[dt - 1], SHARE + dt - 1, (g, to_t))
        c.start()
        share_copies.append(c)
    share = jnp.dot(ctx_s[...], wo_s[t], preferred_element_type=F32)
    for w in both:
        w.second_forward(-1)
    for w in both:
        w.second_forward(1)
    for w in both:
        w.second_forward(2)
    for dt in (2, 1, 3):
        remote(send_buf.at[dt - 1], r_buf.at[dt - 1], SHARE + dt - 1, (g, t)).wait_recv()
    for i in range(3):
        share = share + r_buf[i].astype(F32)
    attended = share.astype(BF16)
    att_out[...] = attended
    residual = (h_buf[t].astype(F32) + attended.astype(F32)).astype(BF16).astype(F32)
    own_squares = jnp.sum(residual * residual, axis=1, keepdims=True)
    stat_send[...] = jnp.broadcast_to(own_squares, (ROWS, HD))
    stat_copies = []
    for dt in (1, 2, 3):
        c = remote(stat_send, stat_buf.at[dt - 1], STAT + dt - 1, (g, (t + dt) % 4))
        c.start()
        stat_copies.append(c)
    for w in both:
        w.second_far(0)
    for w in both:
        w.second_far(-1)
    for w in both:
        w.second_far(1)
    for dt in (1, 2, 3):
        remote(stat_send, stat_buf.at[dt - 1], STAT + dt - 1, (g, t)).wait_recv()
    square_total = own_squares + stat_buf[0] + stat_buf[1] + stat_buf[2]
    inverse_post = lax.rsqrt(square_total * (1.0 / D) + EPS)
    for j in range(WIDTH // HD):
        gain = pg[pl.ds(t * (WIDTH // HD) + j, 1), :]
        norm_out[:, j * HD : (j + 1) * HD] = (residual[:, j * HD : (j + 1) * HD] * inverse_post * gain).astype(BF16)

    for w in both:
        w.second_far(2)
    for c in line_copies + hidden_copies + slice_copies + partial_copies + keys.started + values.started + share_copies + stat_copies:
        c.wait_send()


def store(*refs):
    sources, targets, sems = refs[:4], refs[4:8], refs[8]
    copies = [pltpu.make_async_copy(a, b, sems.at[i]) for i, (a, b) in enumerate(zip(sources, targets))]
    for c in copies:
        c.start()
    for c in copies:
        c.wait()


def shards(
    hidden_in, cache_lengths, in_gain, post_gain, w_query, b_query, b_key, b_value, w_out,
    key_cache, value_cache, next_key_weight, next_w_value,
):
    hbm = pl.BlockSpec(memory_space=pltpu.HBM)
    vmem = pl.BlockSpec(memory_space=pltpu.VMEM)
    operands = (
        hidden_in,
        cache_lengths,
        in_gain.reshape(D // HD, HD),
        post_gain.reshape(D // HD, HD),
        w_query,
        b_query.reshape(HEADS, HD),
        b_key.reshape(1, HD),
        b_value.reshape(1, HD),
        w_out,
        key_cache.reshape(ROWS, CACHE, HD),
        value_cache.reshape(ROWS, CACHE, HD),
        next_key_weight,
        next_w_value,
    )
    attended, normed, key_out, value_out = pl.pallas_call(
        kernel,
        out_shape=[
            pltpu.VMEM((ROWS, WIDTH), BF16),
            pltpu.VMEM((ROWS, WIDTH), BF16),
            pltpu.VMEM((2, 4, 4, BLOCK, HD), BF16),
            pltpu.VMEM((2, 4, 4, BLOCK, HD), BF16),
        ],
        in_specs=[hbm] * 13,
        out_specs=[vmem] * 4,
        scratch_shapes=[
            pltpu.VMEM((4, ROWS, WIDTH), BF16),
            pltpu.SMEM((ROWS,), jnp.int32),
            pltpu.VMEM((D // HD, HD), F32),
            pltpu.VMEM((D // HD, HD), F32),
            pltpu.VMEM((HEADS, HD), F32),
            pltpu.VMEM((1, HD), F32),
            pltpu.VMEM((1, HD), F32),
            pltpu.VMEM((2, 2, 4, SHARD, HD), BF16),
            pltpu.VMEM((CHUNKS, CHUNK, HEADS * HD), BF16),
            pltpu.VMEM((ROWS, CACHE, HD), BF16),
            pltpu.VMEM((ROWS, CACHE, HD), BF16),
            pltpu.VMEM((4, HEADS * HD, WIDTH), BF16),
            pltpu.VMEM((2, 4, ROWS, CHUNK), BF16),
            pltpu.VMEM((4, ROWS, 2 * CHUNK), BF16),
            pltpu.VMEM((4, 2, ROWS, CHUNK), BF16),
            pltpu.VMEM((4, ROWS, 2 * CHUNK), BF16),
            pltpu.VMEM((4, ROWS, HD), F32),
            pltpu.VMEM((4, ROWS, HD), F32),
            pltpu.VMEM((3, ROWS, HD), F32),
            pltpu.VMEM((3, ROWS, HD), F32),
            pltpu.VMEM((ROWS, 8, HD), F32),
            pltpu.VMEM((ROWS, 8, HD), F32),
            pltpu.VMEM((ROWS, 8, HD), F32),
            pltpu.VMEM((ROWS, 8, HD), F32),
            pltpu.VMEM((ROWS, HEADS * HD), BF16),
            pltpu.VMEM((3, ROWS, WIDTH), BF16),
            pltpu.VMEM((3, ROWS, WIDTH), BF16),
            pltpu.VMEM((ROWS, HD), F32),
            pltpu.VMEM((3, ROWS, HD), F32),
            pltpu.SemaphoreType.DMA((LOCALS,)),
            pltpu.SemaphoreType.DMA((COPIES,)),
            pltpu.SemaphoreType.DMA((COPIES,)),
        ],
        compiler_params=pltpu.CompilerParams(
            collective_id=0, has_side_effects=True, vmem_limit_bytes=48 * 1024 * 1024
        ),
        name="decode",
    )(*[pltpu.with_memory_space_constraint(a, pltpu.HBM) for a in operands])
    results = (attended, normed, key_out.reshape(D, HD), value_out.reshape(D, HD))
    return pl.pallas_call(
        store,
        out_shape=[jax.ShapeDtypeStruct(a.shape, a.dtype) for a in results],
        in_specs=[pl.BlockSpec(memory_space=pltpu.VMEM)] * 4,
        out_specs=[hbm] * 4,
        scratch_shapes=[pltpu.SemaphoreType.DMA((4,))],
        name="store",
    )(*[pltpu.with_memory_space_constraint(a, pltpu.VMEM) for a in results])


def solution(mesh):
    in_specs = (
        P("grp", "tp"),
        P("grp"),
        P(),
        P(),
        P(None, "tp"),
        P("tp"),
        P("tp"),
        P("tp"),
        P("tp", None),
        P("grp", "tp", None, None),
        P("grp", "tp", None, None),
        P(("grp", "tp"), None),
        P(("grp", "tp"), None),
    )
    out_specs = (P("grp", "tp"), P("grp", "tp"), P(None, "tp"), P(None, "tp"))
    return jax.shard_map(shards, mesh=mesh, in_specs=in_specs, out_specs=out_specs, check_vma=False)
```

```python
import functools
import math

import jax
import jax.numpy as jnp
from jax import lax
from jax.experimental import pallas as pl
from jax.experimental.pallas import tpu as pltpu
from jax.sharding import PartitionSpec as P

MESH = pl.DeviceIdType.MESH
F32 = jnp.float32
BF16 = jnp.bfloat16

D = 5120
HD = 128
ROWS = 16
HEADS = 5
CACHE = 1280
WIDTH = 1280
SHARD = 40
BLOCK = 160
CHUNK = 640
CHUNKS = 8
EPS = 1e-06
ROPE_BASE = 1000000.0
SCALE = HD ** (-0.5)

HIDDEN = 0
LINE = 3
GATHER = 17
SHARE = 63
STAT = 67
SLICE = 69
TWIN = 75
PARTIAL = 81
COPIES = 87
L_HID, L_LEN, L_IN, L_POST, L_BQ, L_BK, L_BV, L_OWNK, L_OWNV = range(9)
L_WQ = 9
L_KC = L_WQ + CHUNKS
L_VC = L_KC + 8
L_WO = L_VC + 8
LOCALS = L_WO + 4


def kernel(
    hid, lens, in_gain, post_gain, wq, bq, bk, bv, wo, kc, vc, nk, nv,
    att_out, norm_out, k_out, v_out,
    h_buf, len_s, ig, pg, bq_s, bk_s, bv_s, x_buf, wq_s, kc_s, vc_s, wo_s,
    n_buf, n2_buf, nz_buf, ny_buf, pk_send, pv_send, pk_buf, pv_buf,
    q_s, o_s, m_s, l_s, ctx_s, send_buf, r_buf, stat_send, stat_buf,
    lsem, ssem, rsem,
):
    g = lax.axis_index("grp")
    t = lax.axis_index("tp")
    xh, z, y = g // 16, (g // 4) % 4, g % 4

    def group(xh_, z_, y_):
        return xh_ * 16 + z_ * 4 + y_

    def local(src, dst, i):
        return pltpu.make_async_copy(src, dst, lsem.at[i])

    def remote(src, dst, i, dev):
        return pltpu.make_async_remote_copy(
            src_ref=src, dst_ref=dst, send_sem=ssem.at[i], recv_sem=rsem.at[i], device_id=dev, device_id_type=MESH
        )

    columns = pl.ds(pl.multiple_of(t * HD, HD), HD)
    local(hid, h_buf.at[t], L_HID).start()
    local(nk.at[:, columns], x_buf.at[0, xh, t], L_OWNK).start()
    local(nv.at[:, columns], x_buf.at[1, xh, t], L_OWNV).start()
    small = [
        local(lens, len_s, L_LEN),
        local(in_gain, ig, L_IN),
        local(post_gain, pg, L_POST),
        local(bq, bq_s, L_BQ),
        local(bk, bk_s, L_BK),
        local(bv, bv_s, L_BV),
    ]
    for c in small:
        c.start()

    line = [(dx, dt) for dx in (1, 0) for dt in range(4) if (dx, dt) != (0, 0)]
    barrier = pltpu.get_barrier_semaphore()
    partners = [(group((xh + dx) % 2, z, y), (t + dt) % 4) for dx, dt in line]
    partners += [(group(xh, z, (y + d) % 4), t) for d in (1, 2, 3)]
    partners += [(group(xh, (z + d) % 4, y), t) for d in (1, 2, 3)]
    for dev in partners:
        pl.semaphore_signal(barrier, inc=1, device_id=dev, device_id_type=MESH)

    def wq_copy(i):
        return local(wq.at[pl.ds(i * CHUNK, CHUNK)], wq_s.at[i], L_WQ + i)

    def kc_copy(p):
        return local(kc.at[pl.ds(2 * p, 2)], kc_s.at[pl.ds(2 * p, 2)], L_KC + p)

    def vc_copy(p):
        return local(vc.at[pl.ds(2 * p, 2)], vc_s.at[pl.ds(2 * p, 2)], L_VC + p)

    def wo_copy(i):
        return local(wo.at[:, pl.ds(pl.multiple_of(i * WIDTH, WIDTH), WIDTH)], wo_s.at[i], L_WO + i)

    pl.semaphore_wait(barrier, len(partners))

    far_t, twin_t = (t + 2) % 4, t + 1 - 2 * (t % 2)
    far_twin = (twin_t + 2) % 4
    hidden_copies = [
        remote(hid, h_buf.at[t], HIDDEN, (g, far_t)),
        remote(hid, h_buf.at[t], HIDDEN + 1, (g, twin_t)),
    ]
    for c in hidden_copies:
        c.start()
    line_copies = []
    for n, (dx, dt) in enumerate(line):
        to_t = (t + dt) % 4
        dev = (group((xh + dx) % 2, z, y), to_t)
        cols = pl.ds(pl.multiple_of(to_t * HD, HD), HD)
        for kv, src in ((0, nk), (1, nv)):
            c = remote(src.at[:, cols], x_buf.at[kv, xh, t], LINE + 2 * n + kv, dev)
            c.start()
            line_copies.append(c)
    def start_all(make, count):
        def body(i, _):
            make(i).start()
            return 0

        lax.fori_loop(0, count, body, 0)

    start_all(wq_copy, CHUNKS)
    start_all(kc_copy, 8)
    start_all(vc_copy, 8)
    start_all(wo_copy, 4)

    for c in small:
        c.wait()
    row_ids = lax.broadcasted_iota(jnp.int32, (ROWS, HD), 0)
    lane_ids = lax.broadcasted_iota(jnp.int32, (ROWS, HD), 1)
    position = jnp.zeros((ROWS, HD), jnp.int32)
    for r in range(ROWS):
        position = jnp.where(row_ids == r, len_s[r], position)
    exponent = (lane_ids % (HD // 2)).astype(F32) * (-2.0 / HD * math.log(ROPE_BASE))
    angle = position.astype(F32) * jnp.exp(exponent)
    cosine = jnp.cos(angle)
    sine = jnp.where(lane_ids < HD // 2, -jnp.sin(angle), jnp.sin(angle))

    def rotate(v):
        return v * cosine + pltpu.roll(v, HD // 2, 1) * sine

    local(hid, h_buf.at[t], L_HID).wait()
    remote(hid, h_buf.at[far_t], HIDDEN, (g, t)).wait_recv()
    relay = remote(h_buf.at[far_t], h_buf.at[far_t], HIDDEN + 2, (g, twin_t))
    relay.start()
    hidden_copies.append(relay)
    remote(hid, h_buf.at[twin_t], HIDDEN + 1, (g, t)).wait_recv()
    remote(hid, h_buf.at[far_twin], HIDDEN + 2, (g, t)).wait_recv()
    squares = jnp.zeros((ROWS, HD), F32)
    for i in range(4):
        for j in range(WIDTH // HD):
            v = h_buf[i, :, j * HD : (j + 1) * HD].astype(F32)
            squares = squares + v * v
    inverse = lax.rsqrt(jnp.sum(squares, axis=1, keepdims=True) * (1.0 / D) + EPS)
    for i in range(CHUNKS):
        for j in range(CHUNK // HD):
            c = (i % 2) * (CHUNK // HD) + j
            v = h_buf[i // 2, :, c * HD : (c + 1) * HD].astype(F32)
            k = i * (CHUNK // HD) + j
            n_buf[i // 4, i % 4, :, j * HD : (j + 1) * HD] = (v * inverse * ig[k : k + 1, :]).astype(BF16)

    for b in range(4):
        for a in (0, 1):
            n2_buf[b, a] = jnp.concatenate(
                [n_buf[a, i, :, b * BLOCK : (b + 1) * BLOCK].astype(F32) for i in range(4)], axis=1
            ).astype(BF16)
    nz_buf[z] = n_buf[:, z]
    ny_buf[y] = n2_buf[y]
    core = t % 2
    slice_copies = []
    for d in (1, 2, 3):
        zz, yy = (z + d) % 4, (y + d) % 4
        slice_copies.append(
            remote(n_buf.at[core, zz], nz_buf.at[z, core], SLICE + d - 1, (group(xh, zz, y), t))
        )
        slice_copies.append(
            remote(n2_buf.at[yy, core], ny_buf.at[y, core], SLICE + d + 2, (group(xh, z, yy), t))
        )
    for c in slice_copies:
        c.start()

    local(nk.at[:, columns], x_buf.at[0, xh, t], L_OWNK).wait()
    local(nv.at[:, columns], x_buf.at[1, xh, t], L_OWNV).wait()
    for n, (dx, dt) in enumerate(line):
        for kv, src in ((0, nk), (1, nv)):
            land = x_buf.at[kv, (xh - dx + 2) % 2, (t - dt + 4) % 4]
            remote(src.at[:, columns], land, LINE + 2 * n + kv, (g, t)).wait_recv()
    for kv, out in ((0, k_out), (1, v_out)):
        for i in (0, 1):
            out[i, z, y] = x_buf[kv, i].astype(F32).reshape(BLOCK, HD).astype(BF16)

    class Gather:
        def __init__(self, buf, first, second, at, base):
            self.buf, self.a, self.b, self.at, self.base = buf, first, second, at, base
            self.started = []

        def slot(self, da, db, half=None):
            p, q = (self.a + da + 4) % 4, (self.b + db + 4) % 4
            zz, yy = self.at(p, q)
            return self.buf.at[slice(None) if half is None else half, zz, yy]

        def dev(self, da, db):
            zz, yy = self.at((self.a + da + 4) % 4, (self.b + db + 4) % 4)
            return (group(xh, zz, yy), t)

        def send(self, src, i, da, db):
            c = remote(src, src, self.base + i, self.dev(da, db))
            c.start()
            self.started.append(c)

        def recv(self, land, i):
            remote(land, land, self.base + i, (g, t)).wait_recv()

        def first_own(self):
            for i, d in enumerate((1, -1, 2)):
                self.send(self.slot(0, 0), i, d, 0)

        def first_near(self):
            self.recv(self.slot(-1, 0), 0)
            self.recv(self.slot(1, 0), 1)

        def first_far(self):
            self.recv(self.slot(2, 0), 2)

        def second(self, s):
            half = xh if s == 0 else None
            self.send(self.slot(s, 0, half), 4 + 4 * (s % 4), 0, 1)
            self.send(self.slot(s, 0, half), 5 + 4 * (s % 4), 0, -1)
            if s == 2:
                self.send(self.slot(2, 0), 14, 0, 2)

        def piece(self, s, db, part):
            if s == 0:
                return self.slot(0, db, xh).at[pl.ds(part * (BLOCK // 2), BLOCK // 2)]
            return self.slot(s, db, part)

        def second_forward(self, s):
            i = 4 + 4 * (s % 4)
            half = xh if s == 0 else None
            self.recv(self.slot(s, -1, half), i)
            self.send(self.piece(s, -1, 0), i + 2, 0, 1)
            self.recv(self.slot(s, 1, half), i + 1)
            self.send(self.piece(s, 1, 1), i + 3, 0, -1)

        def second_far(self, s):
            i = 4 + 4 * (s % 4)
            if s == 2:
                for k, db in enumerate((-1, 1, 2)):
                    self.recv(self.slot(2, db), i + k)
                return
            self.recv(self.piece(s, 2, 0), i + 2)
            self.recv(self.piece(s, 2, 1), i + 3)

        def cross(self, i, db):
            half = self.slot(0, db, xh)
            c = remote(half, half, self.base + 20 + i, (group(1 - xh, z, y), t))
            c.start()
            self.started.append(c)

        def cross_near(self):
            self.cross(0, -1)
            self.cross(1, 1)

        def cross_far(self):
            self.cross(2, 2)

        def crossed(self):
            for i, db in enumerate((-1, 1, 2)):
                self.recv(self.slot(0, db, 1 - xh), 20 + i)

    keys = Gather(k_out, y, z, lambda p, q: (q, p), GATHER)
    values = Gather(v_out, z, y, lambda p, q: (p, q), GATHER + 23)
    both = (keys, values)
    for w in both:
        w.first_own()

    for i in range(CHUNKS):
        wq_copy(i).wait()
    total = jnp.dot(n_buf[0, 0], wq_s[0], preferred_element_type=F32)
    for i in range(1, CHUNKS):
        total = total + jnp.dot(n_buf[i // 4, i % 4], wq_s[i], preferred_element_type=F32)
    q_s[...] = jnp.zeros_like(q_s)
    for h in range(HEADS):
        v = rotate(total[:, h * HD : (h + 1) * HD] + bq_s[h : h + 1, :])
        q_s[:, h, :] = v.astype(BF16).astype(F32)

    for w in both:
        w.second(0)

    upper = lax.broadcasted_iota(jnp.int32, (16, 1), 0) < 8
    slot_ids = lax.broadcasted_iota(jnp.int32, (16, CACHE), 1)

    def attend(p):
        q2 = q_s[pl.ds(2 * p, 2)].reshape(16, HD)
        left = jnp.concatenate([jnp.where(upper, q2, 0.0), jnp.where(upper, 0.0, q2)], axis=1).astype(BF16)
        right = jnp.concatenate([kc_s[2 * p], kc_s[2 * p + 1]], axis=1)
        scores = lax.dot_general(left, right, (((1,), (1,)), ((), ())), preferred_element_type=F32) * SCALE
        length = jnp.where(upper, len_s[2 * p], len_s[2 * p + 1])
        scores = jnp.where(slot_ids < length, scores, -jnp.inf)
        peak = jnp.max(scores, axis=1, keepdims=True)
        weights = jnp.exp(scores - peak)
        total_weight = jnp.sum(weights, axis=1, keepdims=True)
        mixed = jnp.dot(
            weights.astype(BF16), jnp.concatenate([vc_s[2 * p], vc_s[2 * p + 1]], axis=1), preferred_element_type=F32
        )
        rows = pl.ds(2 * p, 2)
        o_s[rows] = jnp.where(upper, mixed[:, :HD], mixed[:, HD:]).reshape(2, 8, HD)
        m_s[rows] = jnp.broadcast_to(peak, (16, HD)).reshape(2, 8, HD)
        l_s[rows] = jnp.broadcast_to(total_weight, (16, HD)).reshape(2, 8, HD)

    def attend_twice(i, _):
        for p in (2 * i, 2 * i + 1):
            kc_copy(p).wait()
            vc_copy(p).wait()
        for p in (2 * i, 2 * i + 1):
            attend(p)
        return 0

    lax.fori_loop(0, 2, attend_twice, 0)
    twin_copies = []
    for d in (1, 2, 3):
        zz, yy = (z - d + 4) % 4, (y - d + 4) % 4
        for land, i in ((nz_buf.at[zz, core], d - 1), (ny_buf.at[yy, core], d + 2)):
            remote(land, land, SLICE + i, (g, t)).wait_recv()
            c = remote(land, land, TWIN + i, (g, twin_t))
            c.start()
            twin_copies.append(c)
    for w in both:
        w.first_near()
    for w in both:
        w.second(-1)
    attend_twice(2, 0)
    for w in both:
        w.first_far()
    for d in (1, 2, 3):
        zz, yy = (z - d + 4) % 4, (y - d + 4) % 4
        theirs = nz_buf.at[zz, 1 - core]
        remote(theirs, theirs, TWIN + d - 1, (g, t)).wait_recv()
        theirs = ny_buf.at[yy, 1 - core]
        remote(theirs, theirs, TWIN + d + 2, (g, t)).wait_recv()
    key_part = jnp.zeros((4 * ROWS, HD), F32)
    for i in (0, 1):
        key_part = key_part + jnp.dot(
            nz_buf[:, i].reshape(4 * ROWS, CHUNK), k_out[i, z].reshape(CHUNK, HD), preferred_element_type=F32
        )
    pk_send[...] = key_part.reshape(4, ROWS, HD)
    value_part = jnp.zeros((4 * ROWS, HD), F32)
    for i in (0, 1):
        value_part = value_part + jnp.dot(
            ny_buf[:, i].reshape(4 * ROWS, CHUNK), v_out[i, :, y].reshape(CHUNK, HD), preferred_element_type=F32
        )
    pv_send[...] = value_part.reshape(4, ROWS, HD)
    partial_copies = []
    for d in (1, 2, 3):
        zz, yy = (z + d) % 4, (y + d) % 4
        partial_copies.append(remote(pk_send.at[zz], pk_buf.at[d - 1], PARTIAL + d - 1, (group(xh, zz, y), t)))
        partial_copies.append(remote(pv_send.at[yy], pv_buf.at[d - 1], PARTIAL + d + 2, (group(xh, z, yy), t)))
    for c in partial_copies:
        c.start()
    for w in both:
        w.second_forward(0)
    for w in both:
        w.cross_near()
    for w in both:
        w.second(1)
    for w in both:
        w.second(2)
    attend_twice(3, 0)

    for w in both:
        w.second_far(0)
    for w in both:
        w.cross_far()
    for w in both:
        w.second_forward(-1)

    for d in (1, 2, 3):
        remote(pk_send.at[z], pk_buf.at[d - 1], PARTIAL + d - 1, (g, t)).wait_recv()
        remote(pv_send.at[y], pv_buf.at[d - 1], PARTIAL + d + 2, (g, t)).wait_recv()
    key_raw = pk_send[z] + pk_buf[0] + pk_buf[1] + pk_buf[2]
    value_raw = pv_send[y] + pv_buf[0] + pv_buf[1] + pv_buf[2]
    new_key = rotate(key_raw + bk_s[...]).astype(BF16).astype(F32)
    new_value = (value_raw + bv_s[...]).astype(BF16).astype(F32)
    for h in range(HEADS):
        own_score = jnp.sum(q_s[:, h, :] * new_key, axis=1, keepdims=True) * SCALE
        peak = m_s[:, h, :]
        top = jnp.maximum(peak, own_score)
        a = jnp.exp(peak - top)
        b = jnp.exp(own_score - top)
        denominator = a * l_s[:, h, :] + b
        ctx_s[:, h * HD : (h + 1) * HD] = ((a * o_s[:, h, :] + b * new_value) / denominator).astype(BF16)

    for i in range(4):
        wo_copy(i).wait()
    share_copies = []
    share_copies = []

    def share(n, value, to_t):
        send_buf[n] = value.astype(BF16)
        c = remote(send_buf.at[n], r_buf.at[n], SHARE + n, (g, to_t))
        c.start()
        share_copies.append(c)

    def shared(n):
        remote(send_buf.at[n], r_buf.at[n], SHARE + n, (g, t)).wait_recv()
        return r_buf[n].astype(F32)

    def project(b):
        return jnp.dot(ctx_s[...], wo_s[b], preferred_element_type=F32)

    share(0, project(far_twin), twin_t)
    share(1, project(twin_t), twin_t)
    far_sum = project(far_t) + shared(0)
    share(2, far_sum, far_t)
    own_sum = project(t) + shared(1)
    share(3, own_sum, far_t)
    for w in both:
        w.second_forward(1)
    from_far = shared(2)
    also_far = shared(3)
    attended = (own_sum + from_far).astype(BF16)
    att_out[...] = attended
    residual = (h_buf[t].astype(F32) + attended.astype(F32)).astype(BF16).astype(F32)
    far_attended = (far_sum + also_far).astype(BF16).astype(F32)
    far_residual = (h_buf[far_t].astype(F32) + far_attended).astype(BF16).astype(F32)
    own_squares = jnp.sum(residual * residual + far_residual * far_residual, axis=1, keepdims=True)
    stat_send[...] = jnp.broadcast_to(own_squares, (ROWS, HD))
    stat_copies = [remote(stat_send, stat_buf, STAT, (g, twin_t))]
    stat_copies[0].start()
    for w in both:
        w.second_far(-1)
    for w in both:
        w.second_far(1)
    for w in both:
        w.crossed()
    remote(stat_send, stat_buf, STAT, (g, t)).wait_recv()
    square_total = own_squares + stat_buf[...]
    inverse_post = lax.rsqrt(square_total * (1.0 / D) + EPS)
    for j in range(WIDTH // HD):
        gain = pg[pl.ds(t * (WIDTH // HD) + j, 1), :]
        norm_out[:, j * HD : (j + 1) * HD] = (residual[:, j * HD : (j + 1) * HD] * inverse_post * gain).astype(BF16)

    for w in both:
        w.second_far(2)
    for c in line_copies + hidden_copies + slice_copies + twin_copies + partial_copies + keys.started + values.started + share_copies + stat_copies:
        c.wait_send()


def store(*refs):
    sources, targets, sems = refs[:4], refs[4:8], refs[8]
    copies = [pltpu.make_async_copy(a, b, sems.at[i]) for i, (a, b) in enumerate(zip(sources, targets))]
    for c in copies:
        c.start()
    for c in copies:
        c.wait()


def shards(
    hidden_in, cache_lengths, in_gain, post_gain, w_query, b_query, b_key, b_value, w_out,
    key_cache, value_cache, next_key_weight, next_w_value,
):
    hbm = pl.BlockSpec(memory_space=pltpu.HBM)
    vmem = pl.BlockSpec(memory_space=pltpu.VMEM)
    operands = (
        hidden_in,
        cache_lengths,
        in_gain.reshape(D // HD, HD),
        post_gain.reshape(D // HD, HD),
        w_query,
        b_query.reshape(HEADS, HD),
        b_key.reshape(1, HD),
        b_value.reshape(1, HD),
        w_out,
        key_cache.reshape(ROWS, CACHE, HD),
        value_cache.reshape(ROWS, CACHE, HD),
        next_key_weight,
        next_w_value,
    )
    attended, normed, key_out, value_out = pl.pallas_call(
        kernel,
        out_shape=[
            pltpu.VMEM((ROWS, WIDTH), BF16),
            pltpu.VMEM((ROWS, WIDTH), BF16),
            pltpu.VMEM((2, 4, 4, BLOCK, HD), BF16),
            pltpu.VMEM((2, 4, 4, BLOCK, HD), BF16),
        ],
        in_specs=[hbm] * 13,
        out_specs=[vmem] * 4,
        scratch_shapes=[
            pltpu.VMEM((4, ROWS, WIDTH), BF16),
            pltpu.SMEM((ROWS,), jnp.int32),
            pltpu.VMEM((D // HD, HD), F32),
            pltpu.VMEM((D // HD, HD), F32),
            pltpu.VMEM((HEADS, HD), F32),
            pltpu.VMEM((1, HD), F32),
            pltpu.VMEM((1, HD), F32),
            pltpu.VMEM((2, 2, 4, SHARD, HD), BF16),
            pltpu.VMEM((CHUNKS, CHUNK, HEADS * HD), BF16),
            pltpu.VMEM((ROWS, CACHE, HD), BF16),
            pltpu.VMEM((ROWS, CACHE, HD), BF16),
            pltpu.VMEM((4, HEADS * HD, WIDTH), BF16),
            pltpu.VMEM((2, 4, ROWS, CHUNK), BF16),
            pltpu.VMEM((4, 2, ROWS, CHUNK), BF16),
            pltpu.VMEM((4, 2, ROWS, CHUNK), BF16),
            pltpu.VMEM((4, 2, ROWS, CHUNK), BF16),
            pltpu.VMEM((4, ROWS, HD), F32),
            pltpu.VMEM((4, ROWS, HD), F32),
            pltpu.VMEM((3, ROWS, HD), F32),
            pltpu.VMEM((3, ROWS, HD), F32),
            pltpu.VMEM((ROWS, 8, HD), F32),
            pltpu.VMEM((ROWS, 8, HD), F32),
            pltpu.VMEM((ROWS, 8, HD), F32),
            pltpu.VMEM((ROWS, 8, HD), F32),
            pltpu.VMEM((ROWS, HEADS * HD), BF16),
            pltpu.VMEM((4, ROWS, WIDTH), BF16),
            pltpu.VMEM((4, ROWS, WIDTH), BF16),
            pltpu.VMEM((ROWS, HD), F32),
            pltpu.VMEM((ROWS, HD), F32),
            pltpu.SemaphoreType.DMA((LOCALS,)),
            pltpu.SemaphoreType.DMA((COPIES,)),
            pltpu.SemaphoreType.DMA((COPIES,)),
        ],
        compiler_params=pltpu.CompilerParams(
            collective_id=0, has_side_effects=True, vmem_limit_bytes=48 * 1024 * 1024
        ),
        name="decode",
    )(*[pltpu.with_memory_space_constraint(a, pltpu.HBM) for a in operands])
    results = (attended, normed, key_out.reshape(D, HD), value_out.reshape(D, HD))
    return pl.pallas_call(
        store,
        out_shape=[jax.ShapeDtypeStruct(a.shape, a.dtype) for a in results],
        in_specs=[pl.BlockSpec(memory_space=pltpu.VMEM)] * 4,
        out_specs=[hbm] * 4,
        scratch_shapes=[pltpu.SemaphoreType.DMA((4,))],
        name="store",
    )(*[pltpu.with_memory_space_constraint(a, pltpu.VMEM) for a in results])


def solution(mesh):
    in_specs = (
        P("grp", "tp"),
        P("grp"),
        P(),
        P(),
        P(None, "tp"),
        P("tp"),
        P("tp"),
        P("tp"),
        P("tp", None),
        P("grp", "tp", None, None),
        P("grp", "tp", None, None),
        P(("grp", "tp"), None),
        P(("grp", "tp"), None),
    )
    out_specs = (P("grp", "tp"), P("grp", "tp"), P(None, "tp"), P(None, "tp"))
    return jax.shard_map(shards, mesh=mesh, in_specs=in_specs, out_specs=out_specs, check_vma=False)
```

```python
import functools
import math

import jax
import jax.numpy as jnp
from jax import lax
from jax.experimental import pallas as pl
from jax.experimental.pallas import tpu as pltpu
from jax.sharding import PartitionSpec as P

MESH = pl.DeviceIdType.MESH
F32 = jnp.float32
BF16 = jnp.bfloat16

D = 5120
HD = 128
ROWS = 16
HEADS = 5
CACHE = 1280
WIDTH = 1280
SHARD = 40
BLOCK = 160
CHUNK = 640
CHUNKS = 8
EPS = 1e-06
ROPE_BASE = 1000000.0
SCALE = HD ** (-0.5)

HIDDEN = 0
LINE = 3
SHARE = 17
STAT = 21
SLICE = 22
TWIN = 28
PARTIAL = 34
GATHER = 40
EARLY = 9
EACH = EARLY + 32
COPIES = GATHER + 2 * EACH
L_HID, L_LEN, L_IN, L_POST, L_BQ, L_BK, L_BV, L_OWNK, L_OWNV = range(9)
L_WQ = 9
L_KC = L_WQ + CHUNKS
L_VC = L_KC + 8
L_WO = L_VC + 8
LOCALS = L_WO + 4


def kernel(
    hid, lens, in_gain, post_gain, wq, bq, bk, bv, wo, kc, vc, nk, nv,
    att_out, norm_out, k_out, v_out,
    h_buf, len_s, ig, pg, bq_s, bk_s, bv_s, x_buf, wq_s, kc_s, vc_s, wo_s,
    n_buf, n2_buf, nz_buf, ny_buf, pk_send, pv_send, pk_buf, pv_buf,
    q_s, o_s, m_s, l_s, ctx_s, send_buf, r_buf, stat_send, stat_buf,
    lsem, ssem, rsem,
):
    g = lax.axis_index("grp")
    t = lax.axis_index("tp")
    xh, z, y = g // 16, (g // 4) % 4, g % 4

    def group(xh_, z_, y_):
        return xh_ * 16 + z_ * 4 + y_

    def local(src, dst, i):
        return pltpu.make_async_copy(src, dst, lsem.at[i])

    def remote(src, dst, i, dev):
        return pltpu.make_async_remote_copy(
            src_ref=src, dst_ref=dst, send_sem=ssem.at[i], recv_sem=rsem.at[i], device_id=dev, device_id_type=MESH
        )

    columns = pl.ds(pl.multiple_of(t * HD, HD), HD)
    local(hid, h_buf.at[t], L_HID).start()
    local(nk.at[:, columns], x_buf.at[0, xh, t], L_OWNK).start()
    local(nv.at[:, columns], x_buf.at[1, xh, t], L_OWNV).start()
    small = [
        local(lens, len_s, L_LEN),
        local(in_gain, ig, L_IN),
        local(post_gain, pg, L_POST),
        local(bq, bq_s, L_BQ),
        local(bk, bk_s, L_BK),
        local(bv, bv_s, L_BV),
    ]
    for c in small:
        c.start()

    lo, core = t // 2, t % 2
    far_t, twin_t = (t + 2) % 4, t + 1 - 2 * core
    far_twin = (twin_t + 2) % 4
    line = [(xh, twin_t)] + [(1 - xh, b) for b in (t, twin_t, far_t, far_twin)] + [(xh, far_t), (xh, far_twin)]
    barrier = pltpu.get_barrier_semaphore()
    partners = [(group(a, z, y), b) for a, b in line]
    partners += [(group(xh, z, (y + d) % 4), t) for d in (1, 2, 3)]
    partners += [(group(xh, (z + d) % 4, y), t) for d in (1, 2, 3)]
    for dev in partners:
        pl.semaphore_signal(barrier, inc=1, device_id=dev, device_id_type=MESH)

    def wq_copy(i):
        return local(wq.at[pl.ds(i * CHUNK, CHUNK)], wq_s.at[i], L_WQ + i)

    def kc_copy(p):
        return local(kc.at[pl.ds(2 * p, 2)], kc_s.at[pl.ds(2 * p, 2)], L_KC + p)

    def vc_copy(p):
        return local(vc.at[pl.ds(2 * p, 2)], vc_s.at[pl.ds(2 * p, 2)], L_VC + p)

    def wo_copy(i):
        return local(wo.at[:, pl.ds(pl.multiple_of(i * WIDTH, WIDTH), WIDTH)], wo_s.at[i], L_WO + i)

    pl.semaphore_wait(barrier, len(partners))

    hidden_copies = [
        remote(hid, h_buf.at[t], HIDDEN, (g, far_t)),
        remote(hid, h_buf.at[t], HIDDEN + 1, (g, twin_t)),
    ]
    for c in hidden_copies:
        c.start()
    line_copies = []
    for n, (a, b) in enumerate(line):
        cols = pl.ds(pl.multiple_of(b * HD, HD), HD)
        for kv, src in ((0, nk), (1, nv)):
            c = remote(src.at[:, cols], x_buf.at[kv, xh, t], LINE + 2 * n + kv, (group(a, z, y), b))
            c.start()
            line_copies.append(c)
    def start_all(make, count):
        def body(i, _):
            make(i).start()
            return 0

        lax.fori_loop(0, count, body, 0)

    start_all(wq_copy, CHUNKS)
    start_all(kc_copy, 8)
    start_all(vc_copy, 8)
    start_all(wo_copy, 4)

    for c in small:
        c.wait()
    row_ids = lax.broadcasted_iota(jnp.int32, (ROWS, HD), 0)
    lane_ids = lax.broadcasted_iota(jnp.int32, (ROWS, HD), 1)
    position = jnp.zeros((ROWS, HD), jnp.int32)
    for r in range(ROWS):
        position = jnp.where(row_ids == r, len_s[r], position)
    exponent = (lane_ids % (HD // 2)).astype(F32) * (-2.0 / HD * math.log(ROPE_BASE))
    angle = position.astype(F32) * jnp.exp(exponent)
    cosine = jnp.cos(angle)
    sine = jnp.where(lane_ids < HD // 2, -jnp.sin(angle), jnp.sin(angle))

    def rotate(v):
        return v * cosine + pltpu.roll(v, HD // 2, 1) * sine

    class Gather:
        def __init__(self, buf, first, second, at, base):
            self.buf, self.a, self.b, self.at, self.base = buf, first, second, at, base
            self.z, self.y = z, y
            self.started = []

        def slot(self, da, db, half=None):
            p, q = (self.a + da + 4) % 4, (self.b + db + 4) % 4
            zz, yy = self.at(p, q)
            return self.buf.at[slice(None) if half is None else half, zz, yy]

        def dev(self, da, db):
            zz, yy = self.at((self.a + da + 4) % 4, (self.b + db + 4) % 4)
            return (group(xh, zz, yy), t)

        def send(self, src, i, da, db):
            c = remote(src, src, self.base + i, self.dev(da, db))
            c.start()
            self.started.append(c)

        def recv(self, land, i):
            remote(land, land, self.base + i, (g, t)).wait_recv()

        def first_own(self, n, half, rows):
            mine = self.buf.at[half, self.z, self.y, rows]
            for i, d in enumerate((2, 1, -1)):
                self.send(mine, 3 * n + i, d, 0)

        def first_all(self, n, half, rows):
            for i, d in enumerate((2, 1, -1)):
                zz, yy = self.at((self.a - d + 4) % 4, self.b)
                self.recv(self.buf.at[half, zz, yy, rows], 3 * n + i)

        def second(self, s, n, half, rows):
            zz, yy = self.at((self.a + s + 4) % 4, self.b)
            mine = self.buf.at[half, zz, yy, rows]
            i = EARLY + 8 * (s % 4) + 2 * n
            self.send(mine, i, 0, 1)
            self.send(mine, i + 1, 0, -1)

        def second_forward(self, s, blocks):
            i = EARLY + 8 * (s % 4)
            for d in (0, 1):
                step = 2 * d - 1
                zz, yy = self.at((self.a + s + 4) % 4, (self.b + step + 4) % 4)
                for n, (half, rows) in enumerate(blocks):
                    self.recv(self.buf.at[half, zz, yy, rows], i + 2 * n + d)
                self.send(self.slot(s, step, d), i + 6 + d, 0, -step)

        def second_far(self, s):
            i = EARLY + 8 * (s % 4) + 6
            self.recv(self.slot(s, 2, 0), i)
            self.recv(self.slot(s, 2, 1), i + 1)

    keys = Gather(k_out, y, z, lambda p, q: (q, p), GATHER)
    values = Gather(v_out, z, y, lambda p, q: (p, q), GATHER + EACH)
    both = (keys, values)

    chip_rows = pl.ds(pl.multiple_of(lo * (BLOCK // 2), BLOCK // 2), BLOCK // 2)
    next_rows = pl.ds(pl.multiple_of((1 - lo) * (BLOCK // 2), BLOCK // 2), BLOCK // 2)
    own_blocks = ((xh, chip_rows), (xh, next_rows), (1 - xh, slice(None)))

    def arrived(first, last):
        for n in range(first, last):
            for kv in (0, 1):
                land = x_buf.at[kv, line[n][0], line[n][1]]
                remote(land, land, LINE + 2 * n + kv, (g, t)).wait_recv()

    def assemble(a, start, count, rows):
        for kv, out in ((0, k_out), (1, v_out)):
            block = x_buf[kv, a, pl.ds(start, count)].astype(F32).reshape(count * SHARD, HD).astype(BF16)
            out[a, z, y, rows] = block

    def first_own(n):
        for w in both:
            w.first_own(n, *own_blocks[n])

    def first_all(n):
        for w in both:
            w.first_all(n, *own_blocks[n])

    def second(s, n):
        for w in both:
            w.second(s, n, *own_blocks[n])

    def second_forward(s):
        for w in both:
            w.second_forward(s, own_blocks)

    def second_far(s):
        for w in both:
            w.second_far(s)

    local(nk.at[:, columns], x_buf.at[0, xh, t], L_OWNK).wait()
    local(nv.at[:, columns], x_buf.at[1, xh, t], L_OWNV).wait()
    arrived(0, 1)
    assemble(xh, 2 * lo, 2, chip_rows)
    first_own(0)
    second(0, 0)

    local(hid, h_buf.at[t], L_HID).wait()
    remote(hid, h_buf.at[far_t], HIDDEN, (g, t)).wait_recv()
    relay = remote(h_buf.at[far_t], h_buf.at[far_t], HIDDEN + 2, (g, twin_t))
    relay.start()
    hidden_copies.append(relay)
    remote(hid, h_buf.at[twin_t], HIDDEN + 1, (g, t)).wait_recv()
    remote(hid, h_buf.at[far_twin], HIDDEN + 2, (g, t)).wait_recv()
    squares = jnp.zeros((ROWS, HD), F32)
    for i in range(4):
        for j in range(WIDTH // HD):
            v = h_buf[i, :, j * HD : (j + 1) * HD].astype(F32)
            squares = squares + v * v
    inverse = lax.rsqrt(jnp.sum(squares, axis=1, keepdims=True) * (1.0 / D) + EPS)
    for i in range(CHUNKS):
        for j in range(CHUNK // HD):
            c = (i % 2) * (CHUNK // HD) + j
            v = h_buf[i // 2, :, c * HD : (c + 1) * HD].astype(F32)
            k = i * (CHUNK // HD) + j
            n_buf[i // 4, i % 4, :, j * HD : (j + 1) * HD] = (v * inverse * ig[k : k + 1, :]).astype(BF16)

    for b in range(4):
        for a in (0, 1):
            n2_buf[b, a] = jnp.concatenate(
                [n_buf[a, i, :, b * BLOCK : (b + 1) * BLOCK].astype(F32) for i in range(4)], axis=1
            ).astype(BF16)
    nz_buf[z] = n_buf[:, z]
    ny_buf[y] = n2_buf[y]
    slice_copies = []
    for d in (1, 2, 3):
        zz, yy = (z + d) % 4, (y + d) % 4
        slice_copies.append(
            remote(n_buf.at[core, zz], nz_buf.at[z, core], SLICE + d - 1, (group(xh, zz, y), t))
        )
        slice_copies.append(
            remote(n2_buf.at[yy, core], ny_buf.at[y, core], SLICE + d + 2, (group(xh, z, yy), t))
        )
    for c in slice_copies:
        c.start()

    arrived(1, 5)
    assemble(1 - xh, 0, 4, slice(None))
    first_own(2)
    arrived(5, 7)
    assemble(xh, 2 * (1 - lo), 2, next_rows)
    first_own(1)
    second(0, 2)
    second(0, 1)

    for i in range(CHUNKS):
        wq_copy(i).wait()
    total = jnp.dot(n_buf[0, 0], wq_s[0], preferred_element_type=F32)
    for i in range(1, CHUNKS):
        total = total + jnp.dot(n_buf[i // 4, i % 4], wq_s[i], preferred_element_type=F32)
    q_s[...] = jnp.zeros_like(q_s)
    for h in range(HEADS):
        v = rotate(total[:, h * HD : (h + 1) * HD] + bq_s[h : h + 1, :])
        q_s[:, h, :] = v.astype(BF16).astype(F32)

    first_all(0)
    for s in (2, -1, 1):
        second(s, 0)

    upper = lax.broadcasted_iota(jnp.int32, (16, 1), 0) < 8
    slot_ids = lax.broadcasted_iota(jnp.int32, (16, CACHE), 1)

    def attend(p):
        q2 = q_s[pl.ds(2 * p, 2)].reshape(16, HD)
        left = jnp.concatenate([jnp.where(upper, q2, 0.0), jnp.where(upper, 0.0, q2)], axis=1).astype(BF16)
        right = jnp.concatenate([kc_s[2 * p], kc_s[2 * p + 1]], axis=1)
        scores = lax.dot_general(left, right, (((1,), (1,)), ((), ())), preferred_element_type=F32) * SCALE
        length = jnp.where(upper, len_s[2 * p], len_s[2 * p + 1])
        scores = jnp.where(slot_ids < length, scores, -jnp.inf)
        peak = jnp.max(scores, axis=1, keepdims=True)
        weights = jnp.exp(scores - peak)
        total_weight = jnp.sum(weights, axis=1, keepdims=True)
        mixed = jnp.dot(
            weights.astype(BF16), jnp.concatenate([vc_s[2 * p], vc_s[2 * p + 1]], axis=1), preferred_element_type=F32
        )
        rows = pl.ds(2 * p, 2)
        o_s[rows] = jnp.where(upper, mixed[:, :HD], mixed[:, HD:]).reshape(2, 8, HD)
        m_s[rows] = jnp.broadcast_to(peak, (16, HD)).reshape(2, 8, HD)
        l_s[rows] = jnp.broadcast_to(total_weight, (16, HD)).reshape(2, 8, HD)

    def attend_twice(i, _):
        for p in (2 * i, 2 * i + 1):
            kc_copy(p).wait()
            vc_copy(p).wait()
        for p in (2 * i, 2 * i + 1):
            attend(p)
        return 0

    lax.fori_loop(0, 2, attend_twice, 0)
    twin_copies = []
    for d in (1, 2, 3):
        zz, yy = (z - d + 4) % 4, (y - d + 4) % 4
        for land, i in ((nz_buf.at[zz, core], d - 1), (ny_buf.at[yy, core], d + 2)):
            remote(land, land, SLICE + i, (g, t)).wait_recv()
            c = remote(land, land, TWIN + i, (g, twin_t))
            c.start()
            twin_copies.append(c)
    attend_twice(2, 0)
    first_all(2)
    first_all(1)
    for d in (1, 2, 3):
        zz, yy = (z - d + 4) % 4, (y - d + 4) % 4
        theirs = nz_buf.at[zz, 1 - core]
        remote(theirs, theirs, TWIN + d - 1, (g, t)).wait_recv()
        theirs = ny_buf.at[yy, 1 - core]
        remote(theirs, theirs, TWIN + d + 2, (g, t)).wait_recv()
    key_part = jnp.zeros((4 * ROWS, HD), F32)
    for i in (0, 1):
        key_part = key_part + jnp.dot(
            nz_buf[:, i].reshape(4 * ROWS, CHUNK), k_out[i, z].reshape(CHUNK, HD), preferred_element_type=F32
        )
    pk_send[...] = key_part.reshape(4, ROWS, HD)
    value_part = jnp.zeros((4 * ROWS, HD), F32)
    for i in (0, 1):
        value_part = value_part + jnp.dot(
            ny_buf[:, i].reshape(4 * ROWS, CHUNK), v_out[i, :, y].reshape(CHUNK, HD), preferred_element_type=F32
        )
    pv_send[...] = value_part.reshape(4, ROWS, HD)
    partial_copies = []
    for d in (1, 2, 3):
        zz, yy = (z + d) % 4, (y + d) % 4
        partial_copies.append(remote(pk_send.at[zz], pk_buf.at[d - 1], PARTIAL + d - 1, (group(xh, zz, y), t)))
        partial_copies.append(remote(pv_send.at[yy], pv_buf.at[d - 1], PARTIAL + d + 2, (group(xh, z, yy), t)))
    for c in partial_copies:
        c.start()
    for s in (2, -1, 1):
        second(s, 2)
        second(s, 1)
    attend_twice(3, 0)
    second_forward(0)


    for d in (1, 2, 3):
        remote(pk_send.at[z], pk_buf.at[d - 1], PARTIAL + d - 1, (g, t)).wait_recv()
        remote(pv_send.at[y], pv_buf.at[d - 1], PARTIAL + d + 2, (g, t)).wait_recv()
    key_raw = pk_send[z] + pk_buf[0] + pk_buf[1] + pk_buf[2]
    value_raw = pv_send[y] + pv_buf[0] + pv_buf[1] + pv_buf[2]
    new_key = rotate(key_raw + bk_s[...]).astype(BF16).astype(F32)
    new_value = (value_raw + bv_s[...]).astype(BF16).astype(F32)
    for h in range(HEADS):
        own_score = jnp.sum(q_s[:, h, :] * new_key, axis=1, keepdims=True) * SCALE
        peak = m_s[:, h, :]
        top = jnp.maximum(peak, own_score)
        a = jnp.exp(peak - top)
        b = jnp.exp(own_score - top)
        denominator = a * l_s[:, h, :] + b
        ctx_s[:, h * HD : (h + 1) * HD] = ((a * o_s[:, h, :] + b * new_value) / denominator).astype(BF16)

    for i in range(4):
        wo_copy(i).wait()
    share_copies = []
    share_copies = []

    def share(n, value, to_t):
        send_buf[n] = value.astype(BF16)
        c = remote(send_buf.at[n], r_buf.at[n], SHARE + n, (g, to_t))
        c.start()
        share_copies.append(c)

    def shared(n):
        remote(send_buf.at[n], r_buf.at[n], SHARE + n, (g, t)).wait_recv()
        return r_buf[n].astype(F32)

    def project(b):
        return jnp.dot(ctx_s[...], wo_s[b], preferred_element_type=F32)

    share(0, project(far_twin), twin_t)
    share(1, project(twin_t), twin_t)
    second_forward(2)
    far_sum = project(far_t) + shared(0)
    share(2, far_sum, far_t)
    own_sum = project(t) + shared(1)
    share(3, own_sum, far_t)
    second_forward(-1)
    second_forward(1)
    from_far = shared(2)
    also_far = shared(3)
    attended = (own_sum + from_far).astype(BF16)
    att_out[...] = attended
    residual = (h_buf[t].astype(F32) + attended.astype(F32)).astype(BF16).astype(F32)
    far_attended = (far_sum + also_far).astype(BF16).astype(F32)
    far_residual = (h_buf[far_t].astype(F32) + far_attended).astype(BF16).astype(F32)
    own_squares = jnp.sum(residual * residual + far_residual * far_residual, axis=1, keepdims=True)
    stat_send[...] = jnp.broadcast_to(own_squares, (ROWS, HD))
    stat_copies = [remote(stat_send, stat_buf, STAT, (g, twin_t))]
    stat_copies[0].start()
    for s in (0, 2, -1):
        second_far(s)
    remote(stat_send, stat_buf, STAT, (g, t)).wait_recv()
    square_total = own_squares + stat_buf[...]
    inverse_post = lax.rsqrt(square_total * (1.0 / D) + EPS)
    for j in range(WIDTH // HD):
        gain = pg[pl.ds(t * (WIDTH // HD) + j, 1), :]
        norm_out[:, j * HD : (j + 1) * HD] = (residual[:, j * HD : (j + 1) * HD] * inverse_post * gain).astype(BF16)

    second_far(1)
    for c in line_copies + hidden_copies + slice_copies + twin_copies + partial_copies + keys.started + values.started + share_copies + stat_copies:
        c.wait_send()


def store(*refs):
    sources, targets, sems = refs[:4], refs[4:8], refs[8]
    copies = [pltpu.make_async_copy(a, b, sems.at[i]) for i, (a, b) in enumerate(zip(sources, targets))]
    for c in copies:
        c.start()
    for c in copies:
        c.wait()


def shards(
    hidden_in, cache_lengths, in_gain, post_gain, w_query, b_query, b_key, b_value, w_out,
    key_cache, value_cache, next_key_weight, next_w_value,
):
    hbm = pl.BlockSpec(memory_space=pltpu.HBM)
    vmem = pl.BlockSpec(memory_space=pltpu.VMEM)
    operands = (
        hidden_in,
        cache_lengths,
        in_gain.reshape(D // HD, HD),
        post_gain.reshape(D // HD, HD),
        w_query,
        b_query.reshape(HEADS, HD),
        b_key.reshape(1, HD),
        b_value.reshape(1, HD),
        w_out,
        key_cache.reshape(ROWS, CACHE, HD),
        value_cache.reshape(ROWS, CACHE, HD),
        next_key_weight,
        next_w_value,
    )
    attended, normed, key_out, value_out = pl.pallas_call(
        kernel,
        out_shape=[
            pltpu.VMEM((ROWS, WIDTH), BF16),
            pltpu.VMEM((ROWS, WIDTH), BF16),
            pltpu.VMEM((2, 4, 4, BLOCK, HD), BF16),
            pltpu.VMEM((2, 4, 4, BLOCK, HD), BF16),
        ],
        in_specs=[hbm] * 13,
        out_specs=[vmem] * 4,
        scratch_shapes=[
            pltpu.VMEM((4, ROWS, WIDTH), BF16),
            pltpu.SMEM((ROWS,), jnp.int32),
            pltpu.VMEM((D // HD, HD), F32),
            pltpu.VMEM((D // HD, HD), F32),
            pltpu.VMEM((HEADS, HD), F32),
            pltpu.VMEM((1, HD), F32),
            pltpu.VMEM((1, HD), F32),
            pltpu.VMEM((2, 2, 4, SHARD, HD), BF16),
            pltpu.VMEM((CHUNKS, CHUNK, HEADS * HD), BF16),
            pltpu.VMEM((ROWS, CACHE, HD), BF16),
            pltpu.VMEM((ROWS, CACHE, HD), BF16),
            pltpu.VMEM((4, HEADS * HD, WIDTH), BF16),
            pltpu.VMEM((2, 4, ROWS, CHUNK), BF16),
            pltpu.VMEM((4, 2, ROWS, CHUNK), BF16),
            pltpu.VMEM((4, 2, ROWS, CHUNK), BF16),
            pltpu.VMEM((4, 2, ROWS, CHUNK), BF16),
            pltpu.VMEM((4, ROWS, HD), F32),
            pltpu.VMEM((4, ROWS, HD), F32),
            pltpu.VMEM((3, ROWS, HD), F32),
            pltpu.VMEM((3, ROWS, HD), F32),
            pltpu.VMEM((ROWS, 8, HD), F32),
            pltpu.VMEM((ROWS, 8, HD), F32),
            pltpu.VMEM((ROWS, 8, HD), F32),
            pltpu.VMEM((ROWS, 8, HD), F32),
            pltpu.VMEM((ROWS, HEADS * HD), BF16),
            pltpu.VMEM((4, ROWS, WIDTH), BF16),
            pltpu.VMEM((4, ROWS, WIDTH), BF16),
            pltpu.VMEM((ROWS, HD), F32),
            pltpu.VMEM((ROWS, HD), F32),
            pltpu.SemaphoreType.DMA((LOCALS,)),
            pltpu.SemaphoreType.DMA((COPIES,)),
            pltpu.SemaphoreType.DMA((COPIES,)),
        ],
        compiler_params=pltpu.CompilerParams(
            collective_id=0, has_side_effects=True, vmem_limit_bytes=48 * 1024 * 1024
        ),
        name="decode",
    )(*[pltpu.with_memory_space_constraint(a, pltpu.HBM) for a in operands])
    results = (attended, normed, key_out.reshape(D, HD), value_out.reshape(D, HD))
    return pl.pallas_call(
        store,
        out_shape=[jax.ShapeDtypeStruct(a.shape, a.dtype) for a in results],
        in_specs=[pl.BlockSpec(memory_space=pltpu.VMEM)] * 4,
        out_specs=[hbm] * 4,
        scratch_shapes=[pltpu.SemaphoreType.DMA((4,))],
        name="store",
    )(*[pltpu.with_memory_space_constraint(a, pltpu.VMEM) for a in results])


def solution(mesh):
    in_specs = (
        P("grp", "tp"),
        P("grp"),
        P(),
        P(),
        P(None, "tp"),
        P("tp"),
        P("tp"),
        P("tp"),
        P("tp", None),
        P("grp", "tp", None, None),
        P("grp", "tp", None, None),
        P(("grp", "tp"), None),
        P(("grp", "tp"), None),
    )
    out_specs = (P("grp", "tp"), P("grp", "tp"), P(None, "tp"), P(None, "tp"))
    return jax.shard_map(shards, mesh=mesh, in_specs=in_specs, out_specs=out_specs, check_vma=False)
```
